256 devices in a mesh: dp: 32 (over y, x, z_lo), mp: 8 (over z_hi, core).
Axes of the slice: x: 4, y: 4, z: 8 (z_hi: 4, z_lo: 2; z = z_hi * 2 + z_lo), core: 2. Of those that a mesh axis runs over, the one named last changes fastest.
Arguments:
- tokens: bfloat16 [17408, 4096], P('dp'), may hold values from -16 to 16
- out_grad: bfloat16 [17408, 8192], P('dp', 'mp'), may hold values from -64 to 64
- weight: float32 [4096, 8192], P('dp', 'mp'), may hold values from -0.09375 to 0.09375
- momentum: float32 [4096, 8192], P('dp', 'mp'), may hold values from -1.2 to 1.2
- next_tokens: bfloat16 [17408, 4096], P('dp'), may hold values from -6 to 6
Outputs:
- new_weight: float32 [4096, 8192], P('dp', 'mp')
- new_momentum: float32 [4096, 8192], P('dp', 'mp')
- projected: bfloat16 [17408, 8192], P('dp', 'mp')
The draws below stay inside these ranges and needn't reach their ends.
All inputs are finite; a program needn't handle non-finite values.
Results may differ from the reference program's by a relative error of at most 0.0012.
The reference program's roundings to bfloat16 on the way count: a program that leaves them out, or rounds other values in their place, can miss the bound.
Values may be sent and summed in bfloat16 or wider, within the bound.
No kernel may reach another device: no remote copies, remote signals or barrier semaphores. Data moves between devices by JAX's collectives and lax.ppermute only.
A program may use at most 128 MiB of HBM per device.

```python
import jax
import jax.numpy as jnp
from jax import lax

D = 4096
QW = 8192
BLK = 128
TOK_DEV = 544
TOKENS = 17408
LEVELS = 5


def draw_tokens(key, part):
    key = jax.random.fold_in(key, 11)
    noise_key, column_key, row_key, common_key, own_key, amp_key = jax.random.split(key, 6)
    replicas = TOKENS // TOK_DEV
    noise_part = jax.random.normal(noise_key, (TOKENS, D), jnp.float32)
    offset_scale = 0.8
    shared = jax.random.normal(common_key, (1, D), jnp.float32)
    own_part = jax.random.normal(own_key, (replicas, D), jnp.float32)
    amplitude = jnp.exp(jax.random.uniform(amp_key, (replicas, 1), jnp.float32, -0.9, 0.9))
    offsets = offset_scale * amplitude * (0.6 * shared + 0.8 * own_part)
    column = jnp.exp(jax.random.uniform(column_key, (D,), jnp.float32, -1.15, 1.15))
    row_scale = jnp.exp(jax.random.uniform(row_key, (TOKENS, 1), jnp.float32, -0.7, 0.7))
    spread = (noise_part * column[None, :] * row_scale).reshape(replicas, TOK_DEV, D)
    values = (spread + offsets[:, None, :]).reshape(TOKENS, D)
    return jnp.clip(values, -16.0, 16.0).astype(jnp.bfloat16)


def draw_out_grad(key, part):
    key = jax.random.fold_in(key, 23)
    noise_key, column_key, row_key, common_key, amp_key = jax.random.split(key, 5)
    replicas = TOKENS // TOK_DEV
    position = jnp.arange(QW, dtype=jnp.float32) / QW
    noise_part = jax.random.normal(noise_key, (TOKENS, QW), jnp.float32)
    common = 0.25 * jax.random.normal(common_key, (QW,), jnp.float32)
    rising = jnp.exp(1.0986 * position)
    amplitude = jnp.exp(jax.random.uniform(amp_key, (replicas, 1, 1), jnp.float32, -0.5, 0.5))
    column = jnp.exp(jax.random.uniform(column_key, (QW,), jnp.float32, -1.15, 1.15)) * rising
    row_scale = jnp.exp(jax.random.uniform(row_key, (TOKENS, 1), jnp.float32, -0.7, 0.7))
    scaled_noise = (noise_part * row_scale).reshape(replicas, TOK_DEV, QW)
    values = (scaled_noise + amplitude * common[None, None, :]) * column[None, None, :]
    return jnp.clip(values.reshape(TOKENS, QW), -64.0, 64.0).astype(jnp.bfloat16)


def steps_of(stream_key, extent, cuts, smallest, top_value):
    def one(axis_at, blocks):
        heights = jax.random.uniform(jax.random.fold_in(jax.random.fold_in(stream_key, 6), axis_at), (blocks,), jnp.float32, smallest / len(cuts), top_value / len(cuts))
        return jnp.repeat(jnp.exp(heights), extent[axis_at] // blocks).reshape((-1,) + (1,) * (len(extent) - axis_at - 1))

    level = one(*cuts[0])
    for cut in cuts[1:]:
        level = level * one(*cut)
    return level


def normal_values(rng, extent, scale, bound, cuts=(), kind=jnp.bfloat16):
    factor_of = steps_of(rng, extent, cuts, -0.22, 0.18) if cuts else 1.0
    drawn = jax.random.normal(rng, extent, jnp.float32) * scale * factor_of
    return jnp.minimum(jnp.maximum(drawn, -bound), bound).astype(kind)


def setup_inputs(seed: int = 0) -> dict:
    splits = jax.random.split(jax.random.key(seed), 6)
    tokens = draw_tokens(jax.random.fold_in(splits[5], 71), 0)
    out_grad = draw_out_grad(jax.random.fold_in(splits[5], 71), 0)
    weight = normal_values(splits[2], (D, QW), D ** -0.5, 0.09375, ((0, 32), (1, 8)), jnp.float32)
    momentum = normal_values(splits[3], (D, QW), 0.2, 1.2, ((0, 32), (1, 8)), jnp.float32)
    next_tokens = normal_values(splits[4], (TOKENS, D), 1.0, 6.0, ((0, 32),))
    return dict(tokens=tokens, out_grad=out_grad, weight=weight, momentum=momentum, next_tokens=next_tokens)


EPSILON = 1e-6
DECAY = 0.9
STEP_SIZE = 0.005


def combine(lower, upper):
    cross_sum = jnp.sum(lower * upper, axis=(1, 2), keepdims=True)
    lower_norm = jnp.sum(lower * lower, axis=(1, 2), keepdims=True)
    upper_norm = jnp.sum(upper * upper, axis=(1, 2), keepdims=True)
    lower_factor = 1.0 - cross_sum / (2.0 * (lower_norm + EPSILON))
    upper_factor = 1.0 - cross_sum / (2.0 * (upper_norm + EPSILON))
    return lower_factor * lower + upper_factor * upper


def reference(tokens, out_grad, weight, momentum, next_tokens):
    block_count = D // BLK
    replicas = TOKENS // TOK_DEV
    token_blocks = tokens.reshape(replicas, TOK_DEV, block_count, BLK).transpose(2, 0, 1, 3)
    replica_grads = out_grad.reshape(replicas, TOK_DEV, QW).astype(jnp.float32)

    def one_block(block_tokens):
        level_grads = jnp.einsum("rtd,rtq->rdq", block_tokens.astype(jnp.float32), replica_grads, precision=lax.Precision.HIGHEST) / TOK_DEV
        for section_step in range(LEVELS):
            half_count = level_grads.shape[0] // 2
            level_grads = combine(level_grads[:half_count], level_grads[half_count:])
        return level_grads[0]

    combined = lax.map(one_block, token_blocks).reshape(D, QW)
    new_momentum = DECAY * momentum + combined
    new_weight = weight - STEP_SIZE * new_momentum
    weight_half = new_weight.astype(jnp.bfloat16)
    projected = jnp.dot(next_tokens, weight_half, preferred_element_type=jnp.float32).astype(jnp.bfloat16)
    return (new_weight, new_momentum, projected)
```

```python
import functools

import jax
import jax.numpy as jnp
from jax import lax
from jax.experimental import pallas as pl
from jax.experimental.pallas import tpu as pltpu
from jax.sharding import PartitionSpec as P

BLK = 128
EPSILON = 1e-06
DECAY = 0.9
STEP_SIZE = 0.005

NY, NX, NZ, NH, NC = 4, 4, 2, 4, 2
PAIRS_Y = [(0, 0), (1, 1), (2, 2), (3, 3), (0, 2), (1, 3), (0, 1), (0, 3), (1, 2), (2, 3)]
PAIRS_XZ = [(i, j) for i in range(8) for j in range(i, 8)]
F32 = jnp.float32


def move_dp(block, dy=0, dx=0, dz=0):
    route = []
    for y in range(NY):
        for x in range(NX):
            for z in range(NZ):
                target = (((y + dy) % NY) * NX + (x + dx) % NX) * NZ + (z + dz) % NZ
                route.append(((y * NX + x) * NZ + z, target))
    return lax.ppermute(block, "dp", route)


def move_mp(block, dh=0, dc=0):
    route = []
    for h in range(NH):
        for c in range(NC):
            route.append((h * NC + c, ((h + dh) % NH) * NC + (c + dc) % NC))
    return lax.ppermute(block, "mp", route)


def sum_mp(part):
    part = part + move_mp(part, dc=1)
    one, two, three = move_mp(part, dh=1), move_mp(part, dh=2), move_mp(part, dh=3)
    return (part + two) + (one + three)


def turn_kernel(place, tokens_ref, mine_ref, other_ref, turned_ref):
    core = place[2]
    for which, ref in ((0, mine_ref), (1, other_ref)):
        side = core if which == 0 else 1 - core
        own = tokens_ref[:, pl.ds(pl.multiple_of(side * BLK, BLK), BLK)]
        for k, cols in enumerate([own, ref[0, 0], ref[0, 1], ref[0, 2]]):
            turned_ref[k, pl.ds(pl.multiple_of(side * BLK, BLK), BLK), :] = cols.T


def turn(place, tokens, mine, other):
    tok_dev = tokens.shape[0]
    recv = pl.BlockSpec((1, 3, tok_dev, BLK), lambda j, p: (j, 0, 0, 0))
    return pl.pallas_call(
        turn_kernel,
        grid_spec=pltpu.PrefetchScalarGridSpec(
            num_scalar_prefetch=1,
            grid=(NH,),
            in_specs=[
                pl.BlockSpec((tok_dev, 2 * BLK), lambda j, p: (0, p[0] * NH + lax.rem(p[1] - j + NH, NH))),
                recv,
                recv,
            ],
            out_specs=pl.BlockSpec((4, 2 * BLK, tok_dev), lambda j, p: (0, lax.rem(p[1] - j + NH, NH), 0)),
        ),
        out_shape=jax.ShapeDtypeStruct((4, 2 * NH * BLK, tok_dev), jnp.bfloat16),
        compiler_params=pltpu.CompilerParams(vmem_limit_bytes=24 * 2**20),
    )(place, tokens, mine, other)


def grads_kernel(turned_ref, o0_ref, o1_ref, o2_ref, o3_ref, grads_ref, gram_ref, sums_ref):
    step = pl.program_id(0)

    @pl.when(step == 0)
    def _():
        sums_ref[...] = jnp.zeros_like(sums_ref)

    blocks, _, _, span = grads_ref.shape
    for k, o_ref in enumerate((o0_ref, o1_ref, o2_ref, o3_ref)):
        product = jnp.dot(turned_ref[k], o_ref[...], preferred_element_type=F32)
        grads_ref[:, k] = product.reshape(blocks, BLK, span)

    def one_block(m, _):
        sums = [sums_ref[m, n] for n in range(len(PAIRS_Y))]
        for t in range(BLK // 8):
            for part in range(span // 128):
                at, lanes = pl.ds(t * 8, 8), pl.ds(part * 128, 128)
                g = [grads_ref[m, k, at, lanes] for k in range(4)]
                for n, (i, j) in enumerate(PAIRS_Y):
                    sums[n] = sums[n] + g[i] * g[j]
        for n in range(len(PAIRS_Y)):
            sums_ref[m, n] = sums[n]
        return 0

    lax.fori_loop(0, blocks, one_block, 0)

    @pl.when(step == pl.num_programs(0) - 1)
    def _():
        rows = jnp.sum(sums_ref[...], axis=2).reshape(blocks * 16, 128)
        gram_ref[...] = jnp.broadcast_to(jnp.sum(rows.T, axis=0, keepdims=True), gram_ref.shape)


def grads_and_gram(turned, outs):
    tok_dev, cols = outs[0].shape
    span = 256
    blocks = turned.shape[1] // BLK
    out_cols = pl.BlockSpec((tok_dev, span), lambda n: (0, n))
    return pl.pallas_call(
        grads_kernel,
        grid=(cols // span,),
        in_specs=[pl.BlockSpec(turned.shape, lambda n: (0, 0, 0)), out_cols, out_cols, out_cols, out_cols],
        out_specs=[
            pl.BlockSpec((blocks, 4, BLK, span), lambda n: (0, 0, 0, n)),
            pl.BlockSpec((8, 128), lambda n: (0, 0)),
        ],
        out_shape=[
            jax.ShapeDtypeStruct((blocks, 4, BLK, cols), F32),
            jax.ShapeDtypeStruct((8, 128), F32),
        ],
        scratch_shapes=[pltpu.VMEM((blocks, 16, 8, 128), F32)],
        compiler_params=pltpu.CompilerParams(vmem_limit_bytes=48 * 2**20),
    )(turned, *outs)


def mix_kernel(tok_dev, gram_ref, grads_ref, coded_ref):
    step = pl.program_id(0)
    g = gram_ref[...] * (1.0 / (tok_dev * tok_dev))
    at = {}
    for n, pair in enumerate(PAIRS_Y):
        at[pair] = g if n == 0 else pltpu.roll(g, 128 - n, 1)
    p = [at[(k, k)] for k in range(4)]
    c02, c13 = at[(0, 2)], at[(1, 3)]
    a0 = 1.0 - c02 / (2.0 * (p[0] + EPSILON))
    a2 = 1.0 - c02 / (2.0 * (p[2] + EPSILON))
    a1 = 1.0 - c13 / (2.0 * (p[1] + EPSILON))
    a3 = 1.0 - c13 / (2.0 * (p[3] + EPSILON))
    even = jnp.maximum((a0 * a0) * p[0] + 2.0 * ((a0 * a2) * c02) + (a2 * a2) * p[2], 0.0)
    odd = jnp.maximum((a1 * a1) * p[1] + 2.0 * ((a1 * a3) * c13) + (a3 * a3) * p[3], 0.0)
    cross = (a0 * a1) * at[(0, 1)] + (a0 * a3) * at[(0, 3)] + (a2 * a1) * at[(1, 2)] + (a2 * a3) * at[(2, 3)]
    f_even = 1.0 - cross / (2.0 * (even + EPSILON))
    f_odd = 1.0 - cross / (2.0 * (odd + EPSILON))
    w = [f_even * a0, f_odd * a1, f_even * a2, f_odd * a3]
    here = lax.broadcasted_iota(jnp.int32, g.shape, 1) == step * 16
    s = [
        jnp.sum(jnp.where(here, w[k] * (1.0 / tok_dev), 0.0), axis=1, keepdims=True)[:1] for k in range(4)
    ]
    span = 256
    for first in range(0, grads_ref.shape[3], span):
        lanes = pl.ds(first, span)
        mixed = (s[0] * grads_ref[0, 0, :, lanes] + s[2] * grads_ref[0, 2, :, lanes]) + (
            s[1] * grads_ref[0, 1, :, lanes] + s[3] * grads_ref[0, 3, :, lanes]
        )
        peak = jnp.maximum(jnp.max(jnp.abs(mixed), axis=0, keepdims=True), 1e-30)
        exponent = jnp.ceil(jnp.log2(peak))
        mantissa = jnp.ceil(peak * jnp.exp2(-exponent) * 512.0) * (1.0 / 512.0)
        level = mixed * (LEVELS * jnp.exp2(-exponent) / mantissa)
        size = jnp.abs(level)
        whole = jnp.floor(size)
        code = jnp.exp2(whole - 14.0) * (1.0 + (size - whole))
        coded_ref[0, :BLK, lanes] = jnp.where(level < 0.0, -code, code)
        row = lax.broadcasted_iota(jnp.int32, (8, span), 0)
        coded_ref[0, BLK:, lanes] = jnp.where(row == 0, exponent, mantissa)


LEVELS = 29.9


def decode(landed):
    code = landed[:, :BLK].astype(F32)
    exponent = landed[:, BLK : BLK + 1].astype(F32)
    mantissa = landed[:, BLK + 1 : BLK + 2].astype(F32)
    size = jnp.abs(code)
    whole = jnp.floor(jnp.log2(size))
    level = (whole + 13.0) + size * jnp.exp2(-whole)
    return jnp.where(code < 0.0, -level, level) * (jnp.exp2(exponent) * mantissa * (1.0 / LEVELS))


def mix(gram, grads, tok_dev):
    blocks, _, _, cols = grads.shape
    return pl.pallas_call(
        functools.partial(mix_kernel, tok_dev),
        grid=(blocks,),
        in_specs=[
            pl.BlockSpec((8, 128), lambda m: (0, 0)),
            pl.BlockSpec((1, 4, BLK, cols), lambda m: (m, 0, 0, 0)),
        ],
        out_specs=pl.BlockSpec((1, BLK + 8, cols), lambda m: (m, 0, 0)),
        out_shape=jax.ShapeDtypeStruct((blocks, BLK + 8, cols), F32),
        compiler_params=pltpu.CompilerParams(vmem_limit_bytes=56 * 2**20),
    )(gram, grads)


def gram8_kernel(parts_ref, gram_ref):
    def tile(t, sums):
        at = pl.ds(pl.multiple_of(t * 8, 8), 8)
        sums = list(sums)
        for span in range(parts_ref.shape[2] // 128):
            h = [parts_ref[k, at, pl.ds(span * 128, 128)] for k in range(8)]
            for n, (i, j) in enumerate(PAIRS_XZ):
                sums[n] = sums[n] + h[i] * h[j]
        return tuple(sums)

    zero = tuple(jnp.zeros((8, 128), F32) for _ in PAIRS_XZ)
    sums = lax.fori_loop(0, BLK // 8, tile, zero)
    for n, s in enumerate(sums):
        gram_ref[n : n + 1, :] = jnp.sum(s, axis=0, keepdims=True)
    gram_ref[len(sums) :, :] = jnp.zeros((gram_ref.shape[0] - len(sums), 128), F32)


def gram8(parts):
    return pl.pallas_call(
        gram8_kernel,
        out_shape=jax.ShapeDtypeStruct((40, 128), F32),
        compiler_params=pltpu.CompilerParams(vmem_limit_bytes=32 * 2**20),
    )(parts)


def update_kernel(gram_ref, parts_ref, weight_ref, momentum_ref, new_weight_ref, new_momentum_ref, half_ref):
    sums = jnp.sum(gram_ref[...], axis=1, keepdims=True)
    g = {}
    for n, (i, j) in enumerate(PAIRS_XZ):
        g[i, j] = g[j, i] = sums[n : n + 1, :]
    w = [None] * 8
    groups = [[k] for k in range(8)]
    while len(groups) > 1:
        half = len(groups) // 2
        factor = {}
        for a in range(half):
            b = a + half
            factor[a] = 1.0 - g[a, b] / (2.0 * (g[a, a] + EPSILON))
            factor[b] = 1.0 - g[a, b] / (2.0 * (g[b, b] + EPSILON))
        for a, members in enumerate(groups):
            for k in members:
                w[k] = factor[a] if w[k] is None else w[k] * factor[a]
        scaled = {(i, j): (factor[i] * factor[j]) * g[i, j] for i in factor for j in factor}
        g = {}
        for a in range(half):
            for b in range(half):
                total = (scaled[a, b] + scaled[a + half, b + half]) + (scaled[a, b + half] + scaled[a + half, b])
                g[a, b] = jnp.maximum(total, 0.0) if a == b else total
        groups = [groups[a] + groups[a + half] for a in range(half)]
    combined = w[0] * parts_ref[0]
    for k in range(1, 8):
        combined = combined + w[k] * parts_ref[k]
    new_momentum = DECAY * momentum_ref[...] + combined
    new_weight = weight_ref[...] - STEP_SIZE * new_momentum
    new_momentum_ref[...] = new_momentum
    new_weight_ref[...] = new_weight
    half_ref[...] = new_weight.astype(jnp.bfloat16)


def update(gram, parts, weight, momentum):
    rows, cols = weight.shape
    tile = 32
    flat = pl.BlockSpec((tile, cols), lambda t: (t, 0))
    return pl.pallas_call(
        update_kernel,
        grid=(rows // tile,),
        in_specs=[
            pl.BlockSpec(gram.shape, lambda t: (0, 0)),
            pl.BlockSpec((8, tile, cols), lambda t: (0, t, 0)),
            flat,
            flat,
        ],
        out_specs=[flat, flat, flat],
        out_shape=[
            jax.ShapeDtypeStruct((rows, cols), F32),
            jax.ShapeDtypeStruct((rows, cols), F32),
            jax.ShapeDtypeStruct((rows, cols), jnp.bfloat16),
        ],
        compiler_params=pltpu.CompilerParams(vmem_limit_bytes=32 * 2**20),
    )(gram, parts, weight, momentum)


def project_kernel(sets, last, place, left_ref, *refs):
    held, (start_ref, out_ref) = refs[: len(sets)], refs[len(sets) :]
    total = start_ref[...]
    for offsets, ref in zip(sets, held):
        parts = []
        for j, i, e in offsets:
            block = (lax.rem(place[0] - j + NY, NY) * NX + lax.rem(place[1] - i + NX, NX)) * NZ + lax.rem(
                place[2] + e, NZ
            )
            parts.append(left_ref[:, pl.ds(pl.multiple_of(block * BLK, BLK), BLK)])
        total = total + jnp.dot(jnp.concatenate(parts, 1), ref[...], preferred_element_type=F32)
    out_ref[...] = total.astype(out_ref.dtype)


def project(place, left, sets, held, start, last):
    vmem = pl.BlockSpec(memory_space=pltpu.VMEM)
    return pl.pallas_call(
        functools.partial(project_kernel, sets, last),
        in_specs=[pl.BlockSpec(memory_space=pltpu.SMEM)] + [vmem] * (len(held) + 2),
        out_specs=vmem,
        out_shape=jax.ShapeDtypeStruct(start.shape, jnp.bfloat16 if last else F32),
        compiler_params=pltpu.CompilerParams(vmem_limit_bytes=40 * 2**20),
    )(place, left, *held, start)


def gather_and_project(place, own, next_tokens):
    partner = move_dp(own, dz=1)
    a = [own] + [move_dp(own, dx=k) for k in (1, 2, 3)]
    b = [partner] + [move_dp(partner, dy=k) for k in (1, 2, 3)]
    a = jnp.concatenate(a, 0)
    b = jnp.concatenate(b, 0)
    half = a.shape[0] // 2
    a1, a3, b1, b3 = move_dp(a, dy=1), move_dp(a, dy=3), move_dp(b, dx=1), move_dp(b, dx=3)
    row_a = lambda j: [(j, i, 0) for i in range(NX)]
    row_b = lambda i: [(j, i, 1) for j in range(NY)]
    total = jnp.zeros((next_tokens.shape[0], own.shape[1]), F32)
    total = project(place, next_tokens, [row_a(0), row_b(0)], [a, b], total, False)
    a2 = [move_dp(a1[:half], dy=1), move_dp(a3[half:], dy=3)]
    b2 = [move_dp(b1[:half], dx=1), move_dp(b3[half:], dx=3)]
    sets = [row_a(1), row_a(3), row_b(1), row_b(3)]
    total = project(place, next_tokens, sets, [a1, a3, b1, b3], total, False)
    sets = [row_a(2)[:2], row_a(2)[2:], row_b(2)[:2], row_b(2)[2:]]
    return project(place, next_tokens, sets, a2 + b2, total, True)


def shards(tokens, out_grad, weight, momentum, next_tokens):
    dp, mp = lax.axis_index("dp"), lax.axis_index("mp")
    y, x, z = dp // (NX * NZ), dp // NZ % NX, dp % NZ
    tok_dev = tokens.shape[0]
    group = NX * NZ
    sent = []
    for k in (1, 2, 3):
        first = (((y + k) % NY) * group + mp) * BLK
        sent.append(move_dp(lax.dynamic_slice_in_dim(tokens, first, BLK, 1), dy=k))
    outs = [out_grad] + [move_dp(out_grad, dy=k) for k in (1, 2, 3)]
    piece = jnp.stack(sent)
    up, down = move_mp(piece, dh=1), move_mp(piece, dh=3)
    half = tok_dev // 2
    far = jnp.concatenate([move_mp(up[:, :half], dh=1), move_mp(down[:, half:], dh=3)], 1)
    mine = jnp.stack([piece, up, far, down])
    other = move_mp(mine, dc=1)
    place = jnp.stack([y, mp // NC, mp % NC]).astype(jnp.int32)
    grads, gram = grads_and_gram(turn(place, tokens, mine, other), outs)
    coded = mix(sum_mp(gram), grads, tok_dev).astype(jnp.float16)
    rings = [[ring * group + k for k in range(group)] for ring in range(NY)]
    parts = decode(lax.all_to_all(coded, "dp", 0, 0, axis_index_groups=rings))
    new_weight, new_momentum, weight_half = update(sum_mp(gram8(parts)), parts, weight, momentum)
    here = jnp.stack([y, x, z]).astype(jnp.int32)
    projected = gather_and_project(here, weight_half, next_tokens)
    return (new_weight, new_momentum, projected)


def solution(mesh):
    return jax.shard_map(
        shards,
        mesh=mesh,
        in_specs=(P("dp", None), P("dp", "mp"), P("dp", "mp"), P("dp", "mp"), P("dp", None)),
        out_specs=(P("dp", "mp"), P("dp", "mp"), P("dp", "mp")),
        check_vma=False,
    )
```

```python
import functools

import jax
import jax.numpy as jnp
from jax import lax
from jax.experimental import pallas as pl
from jax.experimental.pallas import tpu as pltpu
from jax.sharding import PartitionSpec as P

BLK = 128
EPSILON = 1e-06
DECAY = 0.9
STEP_SIZE = 0.005

NY, NX, NZ, NH, NC = 4, 4, 2, 4, 2
PAIRS_Y = [(0, 0), (1, 1), (2, 2), (3, 3), (0, 2), (1, 3), (0, 1), (0, 3), (1, 2), (2, 3)]
PAIRS_XZ = [(i, j) for i in range(8) for j in range(i, 8)]
F32 = jnp.float32


def move_dp(block, dy=0, dx=0, dz=0):
    route = []
    for y in range(NY):
        for x in range(NX):
            for z in range(NZ):
                target = (((y + dy) % NY) * NX + (x + dx) % NX) * NZ + (z + dz) % NZ
                route.append(((y * NX + x) * NZ + z, target))
    return lax.ppermute(block, "dp", route)


def move_mp(block, dh=0, dc=0):
    route = []
    for h in range(NH):
        for c in range(NC):
            route.append((h * NC + c, ((h + dh) % NH) * NC + (c + dc) % NC))
    return lax.ppermute(block, "mp", route)


def sum_mp(part):
    part = part + move_mp(part, dc=1)
    one, two, three = move_mp(part, dh=1), move_mp(part, dh=2), move_mp(part, dh=3)
    return (part + two) + (one + three)


def turn_kernel(place, tokens_ref, mine_ref, other_ref, turned_ref):
    core = place[2]
    for which, ref in ((0, mine_ref), (1, other_ref)):
        side = core if which == 0 else 1 - core
        own = tokens_ref[:, pl.ds(pl.multiple_of(side * BLK, BLK), BLK)]
        for k, cols in enumerate([own, ref[0, 0], ref[0, 1], ref[0, 2]]):
            turned_ref[k, pl.ds(pl.multiple_of(side * BLK, BLK), BLK), :] = cols.T


def turn(place, tokens, mine, other):
    tok_dev = tokens.shape[0]
    recv = pl.BlockSpec((1, 3, tok_dev, BLK), lambda j, p: (j, 0, 0, 0))
    return pl.pallas_call(
        turn_kernel,
        grid_spec=pltpu.PrefetchScalarGridSpec(
            num_scalar_prefetch=1,
            grid=(NH,),
            in_specs=[
                pl.BlockSpec((tok_dev, 2 * BLK), lambda j, p: (0, p[0] * NH + lax.rem(p[1] - j + NH, NH))),
                recv,
                recv,
            ],
            out_specs=pl.BlockSpec((4, 2 * BLK, tok_dev), lambda j, p: (0, lax.rem(p[1] - j + NH, NH), 0)),
        ),
        out_shape=jax.ShapeDtypeStruct((4, 2 * NH * BLK, tok_dev), jnp.bfloat16),
        compiler_params=pltpu.CompilerParams(vmem_limit_bytes=24 * 2**20),
    )(place, tokens, mine, other)


def grads_kernel(turned_ref, o0_ref, o1_ref, o2_ref, o3_ref, grads_ref, gram_ref, sums_ref):
    step = pl.program_id(0)

    @pl.when(step == 0)
    def _():
        sums_ref[...] = jnp.zeros_like(sums_ref)

    blocks, _, _, span = grads_ref.shape
    for k, o_ref in enumerate((o0_ref, o1_ref, o2_ref, o3_ref)):
        product = jnp.dot(turned_ref[k], o_ref[...], preferred_element_type=F32)
        grads_ref[:, k] = product.reshape(blocks, BLK, span)

    def one_block(m, _):
        sums = [sums_ref[m, n] for n in range(len(PAIRS_Y))]
        for t in range(BLK // 8):
            for part in range(span // 128):
                at, lanes = pl.ds(t * 8, 8), pl.ds(part * 128, 128)
                g = [grads_ref[m, k, at, lanes] for k in range(4)]
                for n, (i, j) in enumerate(PAIRS_Y):
                    sums[n] = sums[n] + g[i] * g[j]
        for n in range(len(PAIRS_Y)):
            sums_ref[m, n] = sums[n]
        return 0

    lax.fori_loop(0, blocks, one_block, 0)

    @pl.when(step == pl.num_programs(0) - 1)
    def _():
        rows = jnp.sum(sums_ref[...], axis=2).reshape(blocks * 16, 128)
        gram_ref[...] = jnp.broadcast_to(jnp.sum(rows.T, axis=0, keepdims=True), gram_ref.shape)


def grads_and_gram(turned, outs):
    tok_dev, cols = outs[0].shape
    span = 256
    blocks = turned.shape[1] // BLK
    out_cols = pl.BlockSpec((tok_dev, span), lambda n: (0, n))
    return pl.pallas_call(
        grads_kernel,
        grid=(cols // span,),
        in_specs=[pl.BlockSpec(turned.shape, lambda n: (0, 0, 0)), out_cols, out_cols, out_cols, out_cols],
        out_specs=[
            pl.BlockSpec((blocks, 4, BLK, span), lambda n: (0, 0, 0, n)),
            pl.BlockSpec((8, 128), lambda n: (0, 0)),
        ],
        out_shape=[
            jax.ShapeDtypeStruct((blocks, 4, BLK, cols), F32),
            jax.ShapeDtypeStruct((8, 128), F32),
        ],
        scratch_shapes=[pltpu.VMEM((blocks, 16, 8, 128), F32)],
        compiler_params=pltpu.CompilerParams(vmem_limit_bytes=48 * 2**20),
    )(turned, *outs)


def mix_kernel(tok_dev, gram_ref, grads_ref, coded_ref):
    step = pl.program_id(0)
    g = gram_ref[...] * (1.0 / (tok_dev * tok_dev))
    at = {}
    for n, pair in enumerate(PAIRS_Y):
        at[pair] = g if n == 0 else pltpu.roll(g, 128 - n, 1)
    p = [at[(k, k)] for k in range(4)]
    c02, c13 = at[(0, 2)], at[(1, 3)]
    a0 = 1.0 - c02 / (2.0 * (p[0] + EPSILON))
    a2 = 1.0 - c02 / (2.0 * (p[2] + EPSILON))
    a1 = 1.0 - c13 / (2.0 * (p[1] + EPSILON))
    a3 = 1.0 - c13 / (2.0 * (p[3] + EPSILON))
    even = jnp.maximum((a0 * a0) * p[0] + 2.0 * ((a0 * a2) * c02) + (a2 * a2) * p[2], 0.0)
    odd = jnp.maximum((a1 * a1) * p[1] + 2.0 * ((a1 * a3) * c13) + (a3 * a3) * p[3], 0.0)
    cross = (a0 * a1) * at[(0, 1)] + (a0 * a3) * at[(0, 3)] + (a2 * a1) * at[(1, 2)] + (a2 * a3) * at[(2, 3)]
    f_even = 1.0 - cross / (2.0 * (even + EPSILON))
    f_odd = 1.0 - cross / (2.0 * (odd + EPSILON))
    w = [f_even * a0, f_odd * a1, f_even * a2, f_odd * a3]
    here = lax.broadcasted_iota(jnp.int32, g.shape, 1) == step * 16
    s = [
        jnp.sum(jnp.where(here, w[k] * (1.0 / tok_dev), 0.0), axis=1, keepdims=True)[:1] for k in range(4)
    ]
    span = 128
    for first in range(0, grads_ref.shape[3], span):
        lanes = pl.ds(first, span)
        mixed = (s[0] * grads_ref[0, 0, :, lanes] + s[2] * grads_ref[0, 2, :, lanes]) + (
            s[1] * grads_ref[0, 1, :, lanes] + s[3] * grads_ref[0, 3, :, lanes]
        )
        peak = jnp.maximum(jnp.max(jnp.abs(mixed), axis=0, keepdims=True), 1e-30)
        exponent = jnp.ceil(jnp.log2(peak))
        mantissa = jnp.ceil(peak * jnp.exp2(-exponent) * 512.0) * (1.0 / 512.0)
        level = mixed * (LEVELS * jnp.exp2(-exponent) / mantissa)
        size = jnp.abs(level)
        whole = jnp.floor(size)
        code = jnp.exp2(whole - 14.0) * (1.0 + (size - whole))
        coded_ref[0, :BLK, lanes] = jnp.where(level < 0.0, -code, code)
        row = lax.broadcasted_iota(jnp.int32, (8, span), 0)
        coded_ref[0, BLK:, lanes] = jnp.where(row == 0, exponent, mantissa)


LEVELS = 29.9


def decode(landed):
    code = landed[:, :BLK].astype(F32)
    exponent = landed[:, BLK : BLK + 1].astype(F32)
    mantissa = landed[:, BLK + 1 : BLK + 2].astype(F32)
    size = jnp.abs(code)
    whole = jnp.floor(jnp.log2(size))
    level = (whole + 13.0) + size * jnp.exp2(-whole)
    return jnp.where(code < 0.0, -level, level) * (jnp.exp2(exponent) * mantissa * (1.0 / LEVELS))


def mix(gram, grads, tok_dev):
    blocks, _, _, cols = grads.shape
    return pl.pallas_call(
        functools.partial(mix_kernel, tok_dev),
        grid=(blocks,),
        in_specs=[
            pl.BlockSpec((8, 128), lambda m: (0, 0)),
            pl.BlockSpec((1, 4, BLK, cols), lambda m: (m, 0, 0, 0)),
        ],
        out_specs=pl.BlockSpec((1, BLK + 8, cols), lambda m: (m, 0, 0)),
        out_shape=jax.ShapeDtypeStruct((blocks, BLK + 8, cols), F32),
        compiler_params=pltpu.CompilerParams(vmem_limit_bytes=56 * 2**20),
    )(gram, grads)


def gram8_kernel(parts_ref, gram_ref):
    def tile(t, sums):
        at = pl.ds(pl.multiple_of(t * 8, 8), 8)
        sums = list(sums)
        for span in range(parts_ref.shape[2] // 128):
            h = [parts_ref[k, at, pl.ds(span * 128, 128)] for k in range(8)]
            for n, (i, j) in enumerate(PAIRS_XZ):
                sums[n] = sums[n] + h[i] * h[j]
        return tuple(sums)

    zero = tuple(jnp.zeros((8, 128), F32) for _ in PAIRS_XZ)
    sums = lax.fori_loop(0, BLK // 8, tile, zero)
    for n, s in enumerate(sums):
        gram_ref[n : n + 1, :] = jnp.sum(s, axis=0, keepdims=True)
    gram_ref[len(sums) :, :] = jnp.zeros((gram_ref.shape[0] - len(sums), 128), F32)


def gram8(parts):
    return pl.pallas_call(
        gram8_kernel,
        out_shape=jax.ShapeDtypeStruct((40, 128), F32),
        compiler_params=pltpu.CompilerParams(vmem_limit_bytes=32 * 2**20),
    )(parts)


def update_kernel(gram_ref, parts_ref, weight_ref, momentum_ref, new_weight_ref, new_momentum_ref, half_ref):
    sums = jnp.sum(gram_ref[...], axis=1, keepdims=True)
    g = {}
    for n, (i, j) in enumerate(PAIRS_XZ):
        g[i, j] = g[j, i] = sums[n : n + 1, :]
    w = [None] * 8
    groups = [[k] for k in range(8)]
    while len(groups) > 1:
        half = len(groups) // 2
        factor = {}
        for a in range(half):
            b = a + half
            factor[a] = 1.0 - g[a, b] / (2.0 * (g[a, a] + EPSILON))
            factor[b] = 1.0 - g[a, b] / (2.0 * (g[b, b] + EPSILON))
        for a, members in enumerate(groups):
            for k in members:
                w[k] = factor[a] if w[k] is None else w[k] * factor[a]
        scaled = {(i, j): (factor[i] * factor[j]) * g[i, j] for i in factor for j in factor}
        g = {}
        for a in range(half):
            for b in range(half):
                total = (scaled[a, b] + scaled[a + half, b + half]) + (scaled[a, b + half] + scaled[a + half, b])
                g[a, b] = jnp.maximum(total, 0.0) if a == b else total
        groups = [groups[a] + groups[a + half] for a in range(half)]
    combined = w[0] * parts_ref[0]
    for k in range(1, 8):
        combined = combined + w[k] * parts_ref[k]
    new_momentum = DECAY * momentum_ref[...] + combined
    new_weight = weight_ref[...] - STEP_SIZE * new_momentum
    new_momentum_ref[...] = new_momentum
    new_weight_ref[...] = new_weight
    half_ref[...] = new_weight.astype(jnp.bfloat16)


def update(gram, parts, weight, momentum):
    rows, cols = weight.shape
    tile = 32
    flat = pl.BlockSpec((tile, cols), lambda t: (t, 0))
    return pl.pallas_call(
        update_kernel,
        grid=(rows // tile,),
        in_specs=[
            pl.BlockSpec(gram.shape, lambda t: (0, 0)),
            pl.BlockSpec((8, tile, cols), lambda t: (0, t, 0)),
            flat,
            flat,
        ],
        out_specs=[flat, flat, flat],
        out_shape=[
            jax.ShapeDtypeStruct((rows, cols), F32),
            jax.ShapeDtypeStruct((rows, cols), F32),
            jax.ShapeDtypeStruct((rows, cols), jnp.bfloat16),
        ],
        compiler_params=pltpu.CompilerParams(vmem_limit_bytes=32 * 2**20),
    )(gram, parts, weight, momentum)


def depth_block(place, j, i, e):
    y, x, z = place[0], place[1], place[2]
    return (lax.rem(y - j + NY, NY) * NX + lax.rem(x - i + NX, NX)) * NZ + lax.rem(z + e, NZ)


def project_kernel(units, last, place, *refs):
    mine, other = refs[:NX], refs[NX : 2 * NX]
    held, start_ref = refs[2 * NX : 2 * NX + units], refs[2 * NX + units]
    rest = refs[2 * NX + units + 1 :]
    total_ref = rest[-1] if last else rest[0]
    step = pl.program_id(0)

    @pl.when(step == 0)
    def _():
        total_ref[...] = start_ref[...]

    unit = held[0][...]
    for u in range(1, units):
        unit = jnp.where(step == u, held[u][...], unit)
    rows = total_ref.shape[1]
    for side, refs_of in enumerate((mine, other)):
        left = jnp.concatenate([ref[...] for ref in refs_of], 1)
        total_ref[side] += jnp.dot(left, unit, preferred_element_type=F32)

    if last:

        @pl.when(step == units - 1)
        def _():
            part = rows // NX
            for k in range(NX):
                first = pl.multiple_of(lax.rem(place[1] + k, NX) * part, part)
                rest[k][...] = total_ref[:, pl.ds(first, part), :].astype(rest[k].dtype)


def project(place, mine, other, held, start, first, stride, last):
    units = len(held)
    rows, cols = start.shape[1:]
    left = [
        pl.BlockSpec(
            (rows, BLK),
            lambda u, p, i=i: (0, depth_block(p, first[0] + u * stride[0], i, first[1] + u * stride[1])),
        )
        for i in range(NX)
    ]
    whole = lambda shape: pl.BlockSpec(shape, lambda u, p: (0,) * len(shape))
    part = (2, rows // NX, cols)
    return pl.pallas_call(
        functools.partial(project_kernel, units, last),
        grid_spec=pltpu.PrefetchScalarGridSpec(
            num_scalar_prefetch=1,
            grid=(units,),
            in_specs=left + left + [whole(h.shape) for h in held] + [whole(start.shape)],
            out_specs=[whole(part)] * NX if last else whole(start.shape),
            scratch_shapes=[pltpu.VMEM(start.shape, F32)] if last else [],
        ),
        out_shape=[jax.ShapeDtypeStruct(part, jnp.bfloat16)] * NX if last else jax.ShapeDtypeStruct(start.shape, F32),
        compiler_params=pltpu.CompilerParams(vmem_limit_bytes=40 * 2**20),
    )(place, *([mine] * NX), *([other] * NX), *held, start)


def assemble_kernel(place, p0_ref, p1_ref, p2_ref, p3_ref, out_ref):
    _, part, cols = p0_ref.shape
    for k, ref in enumerate((p0_ref, p1_ref, p2_ref, p3_ref)):
        column = pl.multiple_of(lax.rem(place[1] - k + NX, NX) * cols, cols)
        for side in range(2):
            core = place[3] if side == 0 else 1 - place[3]
            row = pl.multiple_of(core * part, 16)
            out_ref[pl.ds(row, part), pl.ds(column, cols)] = ref[side]


def assemble(place, parts):
    _, part, cols = parts[0].shape
    return pl.pallas_call(
        assemble_kernel,
        in_specs=[pl.BlockSpec(memory_space=pltpu.SMEM)] + [pl.BlockSpec(memory_space=pltpu.VMEM)] * NX,
        out_specs=pl.BlockSpec(memory_space=pltpu.VMEM),
        out_shape=jax.ShapeDtypeStruct((2 * part, NX * cols), jnp.bfloat16),
    )(place, *parts)


def gather_and_project(place, own, mine, other):
    cols = own.shape[1] // NX
    x = place[1]
    pieces = [lax.dynamic_slice_in_dim(own, ((x + k) % NX) * cols, cols, 1) for k in range(NX)]
    unit = jnp.concatenate([pieces[0]] + [move_dp(pieces[k], dx=k) for k in (1, 2, 3)], 0)
    partner = move_dp(unit, dz=1)
    own_ring = [move_dp(unit, dy=k) for k in (1, 2, 3)]
    own_ring, partner = lax.optimization_barrier((own_ring, partner))
    far_ring = [move_dp(partner, dy=k) for k in (1, 2, 3)]
    total = jnp.zeros((2, mine.shape[0], cols), F32)
    total = project(place, mine, other, [unit, partner], total, (0, 0), (0, 1), False)
    total = project(place, mine, other, own_ring, total, (1, 0), (1, 0), False)
    total, far_ring = lax.optimization_barrier((total, far_ring))
    parts = project(place, mine, other, far_ring, total, (1, 1), (1, 0), True)
    return assemble(place, [parts[0]] + [move_dp(parts[k], dx=k) for k in (1, 2, 3)])


def shards(tokens, out_grad, weight, momentum, next_tokens):
    dp, mp = lax.axis_index("dp"), lax.axis_index("mp")
    y, x, z = dp // (NX * NZ), dp // NZ % NX, dp % NZ
    tok_dev = tokens.shape[0]
    group = NX * NZ
    here = jnp.stack([y, x, z, mp % NC]).astype(jnp.int32)
    next_half = lax.dynamic_slice_in_dim(next_tokens, (mp % NC) * (tok_dev // 2), tok_dev // 2, 0)
    x_rings = [[(a * NX + k) * NZ + b for k in range(NX)] for a in range(NY) for b in range(NZ)]
    next_mine = lax.all_gather(next_half, "dp", axis_index_groups=x_rings, tiled=True)
    sent = []
    for k in (1, 2, 3):
        first = (((y + k) % NY) * group + mp) * BLK
        sent.append(move_dp(lax.dynamic_slice_in_dim(tokens, first, BLK, 1), dy=k))
    sent, out_grad = lax.optimization_barrier((sent, out_grad))
    outs = [move_dp(out_grad, dy=k) for k in (1, 2, 3)]
    piece = jnp.stack(sent)
    up, down = move_mp(piece, dh=1), move_mp(piece, dh=3)
    half = tok_dev // 2
    far = jnp.concatenate([move_mp(up[:, :half], dh=1), move_mp(down[:, half:], dh=3)], 1)
    up, down, far, outs = lax.optimization_barrier((up, down, far, outs))
    mine = jnp.stack([piece, up, far, down])
    other = move_mp(mine, dc=1)
    place = jnp.stack([y, mp // NC, mp % NC]).astype(jnp.int32)
    grads, gram = grads_and_gram(turn(place, tokens, mine, other), [out_grad] + outs)
    coded = mix(sum_mp(gram), grads, tok_dev).astype(jnp.float16)
    rings = [[ring * group + k for k in range(group)] for ring in range(NY)]
    coded, next_mine = lax.optimization_barrier((coded, next_mine))
    next_other = move_mp(next_mine, dc=1)
    landed = lax.all_to_all(coded, "dp", 0, 0, axis_index_groups=rings)
    landed, next_other = lax.optimization_barrier((landed, next_other))
    parts = decode(landed)
    new_weight, new_momentum, weight_half = update(sum_mp(gram8(parts)), parts, weight, momentum)
    projected = gather_and_project(here, weight_half, next_mine, next_other)
    return (new_weight, new_momentum, projected)


def solution(mesh):
    return jax.shard_map(
        shards,
        mesh=mesh,
        in_specs=(P("dp", None), P("dp", "mp"), P("dp", "mp"), P("dp", "mp"), P("dp", None)),
        out_specs=(P("dp", "mp"), P("dp", "mp"), P("dp", "mp")),
        check_vma=False,
    )
```

```python
import functools

import jax
import jax.numpy as jnp
from jax import lax
from jax.experimental import pallas as pl
from jax.experimental.pallas import tpu as pltpu
from jax.sharding import PartitionSpec as P

BLK = 128
EPSILON = 1e-06
DECAY = 0.9
STEP_SIZE = 0.005

NY, NX, NZ, NH, NC = 4, 4, 2, 4, 2
PAIRS_Y = [(0, 0), (1, 1), (2, 2), (3, 3), (0, 2), (1, 3), (0, 1), (0, 3), (1, 2), (2, 3)]
PAIRS_XZ = [(i, j) for i in range(8) for j in range(i, 8)]
F32 = jnp.float32


def move_dp(block, dy=0, dx=0, dz=0):
    route = []
    for y in range(NY):
        for x in range(NX):
            for z in range(NZ):
                target = (((y + dy) % NY) * NX + (x + dx) % NX) * NZ + (z + dz) % NZ
                route.append(((y * NX + x) * NZ + z, target))
    return lax.ppermute(block, "dp", route)


def move_mp(block, dh=0, dc=0):
    route = []
    for h in range(NH):
        for c in range(NC):
            route.append((h * NC + c, ((h + dh) % NH) * NC + (c + dc) % NC))
    return lax.ppermute(block, "mp", route)


def sum_mp(part):
    part = part + move_mp(part, dc=1)
    one, two, three = move_mp(part, dh=1), move_mp(part, dh=2), move_mp(part, dh=3)
    return (part + two) + (one + three)


def grads_kernel(
    place, tokens_ref, mine_ref, other_ref, o0_ref, o1_ref, o2_ref, o2b_ref, o3_ref, grads_ref, gram_ref, turned_ref, sums_ref
):
    step = pl.program_id(0)

    @pl.when(step == 0)
    def _():
        sums_ref[...] = jnp.zeros_like(sums_ref)
        for j in range(NH):
            for which, ref in ((0, mine_ref), (1, other_ref)):
                side = place[4] if which == 0 else 1 - place[4]
                block = lax.rem(place[3] - j + NH, NH) * 2 + side
                at = pl.ds(pl.multiple_of(block * BLK, BLK), BLK)
                for k, cols in enumerate([tokens_ref[:, at], ref[j, 0], ref[j, 1], ref[j, 2]]):
                    turned_ref[k, at, :] = cols.T

    blocks, _, _, span = grads_ref.shape
    o2 = jnp.where(step < pl.num_programs(0) // 2, o2_ref[...], o2b_ref[...])
    for k, out in enumerate((o0_ref[...], o1_ref[...], o2, o3_ref[...])):
        product = jnp.dot(turned_ref[k], out, preferred_element_type=F32)
        grads_ref[:, k] = product.reshape(blocks, BLK, span)

    def one_block(m, _):
        sums = [sums_ref[m, n] for n in range(len(PAIRS_Y))]
        for t in range(BLK // 8):
            for part in range(span // 128):
                at, lanes = pl.ds(t * 8, 8), pl.ds(part * 128, 128)
                g = [grads_ref[m, k, at, lanes] for k in range(4)]
                for n, (i, j) in enumerate(PAIRS_Y):
                    sums[n] = sums[n] + g[i] * g[j]
        for n in range(len(PAIRS_Y)):
            sums_ref[m, n] = sums[n]
        return 0

    lax.fori_loop(0, blocks, one_block, 0)

    @pl.when(step == pl.num_programs(0) - 1)
    def _():
        rows = jnp.sum(sums_ref[...], axis=2).reshape(blocks * 16, 128)
        gram_ref[...] = jnp.broadcast_to(jnp.sum(rows.T, axis=0, keepdims=True), gram_ref.shape)


def grads_and_gram(place, tokens, mine, other, outs):
    tok_dev, cols = outs[0].shape
    span = 256
    blocks = NH * NC
    half = cols // span // 2
    out_cols = pl.BlockSpec((tok_dev, span), lambda n, p: (0, n))
    first_half = pl.BlockSpec((tok_dev, span), lambda n, p: (0, jnp.minimum(n, half - 1)))
    last_half = pl.BlockSpec((tok_dev, span), lambda n, p: (0, jnp.maximum(n - half, 0)))
    landed = pl.BlockSpec(mine.shape, lambda n, p: (0, 0, 0, 0))
    return pl.pallas_call(
        grads_kernel,
        grid_spec=pltpu.PrefetchScalarGridSpec(
            num_scalar_prefetch=1,
            grid=(cols // span,),
            in_specs=[pl.BlockSpec((tok_dev, blocks * BLK), lambda n, p: (0, p[0])), landed, landed]
            + [out_cols, out_cols, first_half, last_half, out_cols],
            out_specs=[
                pl.BlockSpec((blocks, 4, BLK, span), lambda n, p: (0, 0, 0, n)),
                pl.BlockSpec((8, 128), lambda n, p: (0, 0)),
            ],
            scratch_shapes=[
                pltpu.VMEM((4, blocks * BLK, tok_dev), jnp.bfloat16),
                pltpu.VMEM((blocks, 16, 8, 128), F32),
            ],
        ),
        out_shape=[
            jax.ShapeDtypeStruct((blocks, 4, BLK, cols), F32),
            jax.ShapeDtypeStruct((8, 128), F32),
        ],
        compiler_params=pltpu.CompilerParams(vmem_limit_bytes=60 * 2**20),
    )(place, tokens, mine, other, outs[0], outs[1], *outs[2], outs[3])


def mix_kernel(tok_dev, gram_ref, grads_ref, coded_ref):
    step = pl.program_id(0)
    g = gram_ref[...] * (1.0 / (tok_dev * tok_dev))
    at = {}
    for n, pair in enumerate(PAIRS_Y):
        at[pair] = g if n == 0 else pltpu.roll(g, 128 - n, 1)
    p = [at[(k, k)] for k in range(4)]
    c02, c13 = at[(0, 2)], at[(1, 3)]
    a0 = 1.0 - c02 / (2.0 * (p[0] + EPSILON))
    a2 = 1.0 - c02 / (2.0 * (p[2] + EPSILON))
    a1 = 1.0 - c13 / (2.0 * (p[1] + EPSILON))
    a3 = 1.0 - c13 / (2.0 * (p[3] + EPSILON))
    even = jnp.maximum((a0 * a0) * p[0] + 2.0 * ((a0 * a2) * c02) + (a2 * a2) * p[2], 0.0)
    odd = jnp.maximum((a1 * a1) * p[1] + 2.0 * ((a1 * a3) * c13) + (a3 * a3) * p[3], 0.0)
    cross = (a0 * a1) * at[(0, 1)] + (a0 * a3) * at[(0, 3)] + (a2 * a1) * at[(1, 2)] + (a2 * a3) * at[(2, 3)]
    f_even = 1.0 - cross / (2.0 * (even + EPSILON))
    f_odd = 1.0 - cross / (2.0 * (odd + EPSILON))
    w = [f_even * a0, f_odd * a1, f_even * a2, f_odd * a3]
    here = lax.broadcasted_iota(jnp.int32, g.shape, 1) == step * 16
    s = [
        jnp.sum(jnp.where(here, w[k] * (1.0 / tok_dev), 0.0), axis=1, keepdims=True)[:1] for k in range(4)
    ]
    span = 128
    for first in range(0, grads_ref.shape[3], span):
        lanes = pl.ds(first, span)
        mixed = (s[0] * grads_ref[0, 0, :, lanes] + s[2] * grads_ref[0, 2, :, lanes]) + (
            s[1] * grads_ref[0, 1, :, lanes] + s[3] * grads_ref[0, 3, :, lanes]
        )
        peak = jnp.maximum(jnp.max(jnp.abs(mixed), axis=0, keepdims=True), 1e-30)
        exponent = jnp.ceil(jnp.log2(peak))
        mantissa = jnp.ceil(peak * jnp.exp2(-exponent) * 512.0) * (1.0 / 512.0)
        level = mixed * (LEVELS * jnp.exp2(-exponent) / mantissa)
        size = jnp.abs(level)
        whole = jnp.floor(size)
        code = jnp.exp2(whole - 14.0) * (1.0 + (size - whole))
        coded_ref[0, :BLK, lanes] = jnp.where(level < 0.0, -code, code)
        row = lax.broadcasted_iota(jnp.int32, (8, span), 0)
        coded_ref[0, BLK:, lanes] = jnp.where(row == 0, exponent, mantissa)


LEVELS = 29.9


def decode(landed):
    code = landed[:, :BLK].astype(F32)
    exponent = landed[:, BLK : BLK + 1].astype(F32)
    mantissa = landed[:, BLK + 1 : BLK + 2].astype(F32)
    size = jnp.abs(code)
    whole = jnp.floor(jnp.log2(size))
    level = (whole + 13.0) + size * jnp.exp2(-whole)
    return jnp.where(code < 0.0, -level, level) * (jnp.exp2(exponent) * mantissa * (1.0 / LEVELS))


def mix(gram, grads, tok_dev):
    blocks, _, _, cols = grads.shape
    return pl.pallas_call(
        functools.partial(mix_kernel, tok_dev),
        grid=(blocks,),
        in_specs=[
            pl.BlockSpec((8, 128), lambda m: (0, 0)),
            pl.BlockSpec((1, 4, BLK, cols), lambda m: (m, 0, 0, 0)),
        ],
        out_specs=pl.BlockSpec((1, BLK + 8, cols), lambda m: (m, 0, 0)),
        out_shape=jax.ShapeDtypeStruct((blocks, BLK + 8, cols), F32),
        compiler_params=pltpu.CompilerParams(vmem_limit_bytes=16 * 2**20),
    )(gram, grads)


def gram8_kernel(parts_ref, gram_ref):
    def tile(t, sums):
        at = pl.ds(pl.multiple_of(t * 8, 8), 8)
        sums = list(sums)
        for span in range(parts_ref.shape[2] // 128):
            h = [parts_ref[k, at, pl.ds(span * 128, 128)] for k in range(8)]
            for n, (i, j) in enumerate(PAIRS_XZ):
                sums[n] = sums[n] + h[i] * h[j]
        return tuple(sums)

    zero = tuple(jnp.zeros((8, 128), F32) for _ in PAIRS_XZ)
    sums = lax.fori_loop(0, BLK // 8, tile, zero)
    for n, s in enumerate(sums):
        gram_ref[n : n + 1, :] = jnp.sum(s, axis=0, keepdims=True)
    gram_ref[len(sums) :, :] = jnp.zeros((gram_ref.shape[0] - len(sums), 128), F32)


def gram8(parts):
    return pl.pallas_call(
        gram8_kernel,
        out_shape=jax.ShapeDtypeStruct((40, 128), F32),
        compiler_params=pltpu.CompilerParams(vmem_limit_bytes=32 * 2**20),
    )(parts)


def update_kernel(gram_ref, parts_ref, weight_ref, momentum_ref, new_weight_ref, new_momentum_ref, half_ref):
    sums = jnp.sum(gram_ref[...], axis=1, keepdims=True)
    g = {}
    for n, (i, j) in enumerate(PAIRS_XZ):
        g[i, j] = g[j, i] = sums[n : n + 1, :]
    w = [None] * 8
    groups = [[k] for k in range(8)]
    while len(groups) > 1:
        half = len(groups) // 2
        factor = {}
        for a in range(half):
            b = a + half
            factor[a] = 1.0 - g[a, b] / (2.0 * (g[a, a] + EPSILON))
            factor[b] = 1.0 - g[a, b] / (2.0 * (g[b, b] + EPSILON))
        for a, members in enumerate(groups):
            for k in members:
                w[k] = factor[a] if w[k] is None else w[k] * factor[a]
        scaled = {(i, j): (factor[i] * factor[j]) * g[i, j] for i in factor for j in factor}
        g = {}
        for a in range(half):
            for b in range(half):
                total = (scaled[a, b] + scaled[a + half, b + half]) + (scaled[a, b + half] + scaled[a + half, b])
                g[a, b] = jnp.maximum(total, 0.0) if a == b else total
        groups = [groups[a] + groups[a + half] for a in range(half)]
    combined = w[0] * parts_ref[0]
    for k in range(1, 8):
        combined = combined + w[k] * parts_ref[k]
    new_momentum = DECAY * momentum_ref[...] + combined
    new_weight = weight_ref[...] - STEP_SIZE * new_momentum
    new_momentum_ref[...] = new_momentum
    new_weight_ref[...] = new_weight
    half_ref[...] = new_weight.astype(jnp.bfloat16)


def update(gram, parts, weight, momentum):
    rows, cols = weight.shape
    tile = 32
    flat = pl.BlockSpec((tile, cols), lambda t: (t, 0))
    return pl.pallas_call(
        update_kernel,
        grid=(rows // tile,),
        in_specs=[
            pl.BlockSpec(gram.shape, lambda t: (0, 0)),
            pl.BlockSpec((8, tile, cols), lambda t: (0, t, 0)),
            flat,
            flat,
        ],
        out_specs=[flat, flat, flat],
        out_shape=[
            jax.ShapeDtypeStruct((rows, cols), F32),
            jax.ShapeDtypeStruct((rows, cols), F32),
            jax.ShapeDtypeStruct((rows, cols), jnp.bfloat16),
        ],
        compiler_params=pltpu.CompilerParams(vmem_limit_bytes=32 * 2**20),
    )(gram, parts, weight, momentum)


def depth_block(place, j, i, e):
    y, x, z = place[0], place[1], place[2]
    return (lax.rem(y - j + NY, NY) * NX + lax.rem(x - i + NX, NX)) * NZ + lax.rem(z + e, NZ)


def project_kernel(units, start, last, place, *refs):
    mine, other = refs[:NX], refs[NX : 2 * NX]
    held, rest = refs[2 * NX : 2 * NX + units], refs[2 * NX + units :]
    total_ref = rest[-1]
    step = pl.program_id(0)

    @pl.when(step == 0)
    def _():
        total_ref[...] = rest[0][...] if start else jnp.zeros_like(total_ref)

    unit = held[0][...]
    for u in range(1, units):
        unit = jnp.where(step == u, held[u][...], unit)
    rows = total_ref.shape[1]
    for side, refs_of in enumerate((mine, other)):
        left = jnp.concatenate([ref[...] for ref in refs_of], 1)
        total_ref[side] += jnp.dot(left, unit, preferred_element_type=F32)

    if last:

        @pl.when(step == units - 1)
        def _():
            part = rows // NX
            for k in range(NX):
                first = pl.multiple_of(lax.rem(place[1] + k, NX) * part, part)
                rest[1 + k][...] = total_ref[:, pl.ds(first, part), :].astype(rest[1 + k].dtype)


def project(place, mine, other, held, start, first, stride, last):
    units = len(held)
    rows, cols = mine.shape[0], held[0].shape[1]
    shape = (2, rows, cols)
    begin = [] if start is None else [start]
    left = [
        pl.BlockSpec(
            (rows, BLK),
            lambda u, p, i=i: (0, depth_block(p, first[0] + u * stride[0], i, first[1] + u * stride[1])),
        )
        for i in range(NX)
    ]
    whole = lambda shape: pl.BlockSpec(shape, lambda u, p: (0,) * len(shape))
    part = (2, rows // NX, cols)
    return pl.pallas_call(
        functools.partial(project_kernel, units, len(begin), last),
        grid_spec=pltpu.PrefetchScalarGridSpec(
            num_scalar_prefetch=1,
            grid=(units,),
            in_specs=left + left + [whole(h.shape) for h in held] + [whole(shape)] * len(begin),
            out_specs=[whole(part)] * NX if last else whole(shape),
            scratch_shapes=[pltpu.VMEM(shape, F32)] if last else [],
        ),
        out_shape=[jax.ShapeDtypeStruct(part, jnp.bfloat16)] * NX if last else jax.ShapeDtypeStruct(shape, F32),
        compiler_params=pltpu.CompilerParams(vmem_limit_bytes=40 * 2**20),
    )(place, *([mine] * NX), *([other] * NX), *held, *begin)


def assemble_kernel(place, p0_ref, p1_ref, p2_ref, p3_ref, out_ref):
    _, part, cols = p0_ref.shape
    for k, ref in enumerate((p0_ref, p1_ref, p2_ref, p3_ref)):
        column = pl.multiple_of(lax.rem(place[1] - k + NX, NX) * cols, cols)
        for side in range(2):
            core = place[4] if side == 0 else 1 - place[4]
            row = pl.multiple_of(core * part, 16)
            out_ref[pl.ds(row, part), pl.ds(column, cols)] = ref[side]


def assemble(place, parts):
    _, part, cols = parts[0].shape
    return pl.pallas_call(
        assemble_kernel,
        in_specs=[pl.BlockSpec(memory_space=pltpu.SMEM)] + [pl.BlockSpec(memory_space=pltpu.VMEM)] * NX,
        out_specs=pl.BlockSpec(memory_space=pltpu.VMEM),
        out_shape=jax.ShapeDtypeStruct((2 * part, NX * cols), jnp.bfloat16),
    )(place, *parts)


def gather_and_project(place, own, mine, other):
    cols = own.shape[1] // NX
    x = place[1]
    pieces = [lax.dynamic_slice_in_dim(own, ((x + k) % NX) * cols, cols, 1) for k in range(NX)]
    unit = jnp.concatenate([pieces[0]] + [move_dp(pieces[k], dx=k) for k in (1, 2, 3)], 0)
    partner = move_dp(unit, dz=1)
    own_ring = [move_dp(unit, dy=k) for k in (1, 2, 3)]
    total = project(place, mine, other, [unit, partner], None, (0, 0), (0, 1), False)
    own_ring, partner, total = lax.optimization_barrier((own_ring, partner, total))
    far_ring = [move_dp(partner, dy=k) for k in (1, 2, 3)]
    total = project(place, mine, other, own_ring, total, (1, 0), (1, 0), False)
    total, far_ring = lax.optimization_barrier((total, far_ring))
    parts = project(place, mine, other, far_ring, total, (1, 1), (1, 0), True)
    return assemble(place, [parts[0]] + [move_dp(parts[k], dx=k) for k in (1, 2, 3)])


def shards(tokens, out_grad, weight, momentum, next_tokens):
    dp, mp = lax.axis_index("dp"), lax.axis_index("mp")
    y, x, z = dp // (NX * NZ), dp // NZ % NX, dp % NZ
    tok_dev = tokens.shape[0]
    group = NX * NZ
    here = jnp.stack([y, x, z, mp // NC, mp % NC]).astype(jnp.int32)
    sent = []
    for k in (1, 2, 3):
        first = (((y + k) % NY) * group + mp) * BLK
        sent.append(lax.dynamic_slice_in_dim(tokens, first, BLK, 1))
    sent, next_tokens = lax.optimization_barrier((sent, next_tokens))
    sent = [move_dp(block, dy=k) for k, block in zip((1, 2, 3), sent)]
    next_half = lax.dynamic_slice_in_dim(next_tokens, (mp % NC) * (tok_dev // 2), tok_dev // 2, 0)
    sent, out_grad, next_half = lax.optimization_barrier((sent, out_grad, next_half))
    x_rings = [[(a * NX + k) * NZ + b for k in range(NX)] for a in range(NY) for b in range(NZ)]
    next_mine = lax.all_gather(next_half, "dp", axis_index_groups=x_rings, tiled=True)
    piece = jnp.stack(sent)
    half, middle = tok_dev // 2, out_grad.shape[1] // 2
    near = [move_dp(out_grad, dy=1), move_dp(out_grad, dy=3)]
    up, down = move_mp(piece, dh=1), move_mp(piece, dh=3)
    near, up, down = lax.optimization_barrier((near, up, down))
    far_out = [move_dp(near[0][:, :middle], dy=1), move_dp(near[1][:, middle:], dy=3)]
    far = [move_mp(up[:, :half], dh=1), move_mp(down[:, half:], dh=3)]
    far, far_out, near = lax.optimization_barrier((far, far_out, near))
    far = jnp.concatenate(far, 1)
    mine = jnp.stack([piece, up, far, down])
    other = move_mp(mine, dc=1)
    grads, gram = grads_and_gram(here, tokens, mine, other, [out_grad, near[0], far_out, near[1]])
    coded = mix(sum_mp(gram), grads, tok_dev).astype(jnp.float16)
    rings = [[ring * group + k for k in range(group)] for ring in range(NY)]
    coded, next_mine = lax.optimization_barrier((coded, next_mine))
    next_other = move_mp(next_mine, dc=1)
    landed = lax.all_to_all(coded, "dp", 0, 0, axis_index_groups=rings)
    landed, next_other = lax.optimization_barrier((landed, next_other))
    parts = decode(landed)
    new_weight, new_momentum, weight_half = update(sum_mp(gram8(parts)), parts, weight, momentum)
    projected = gather_and_project(here, weight_half, next_mine, next_other)
    return (new_weight, new_momentum, projected)


def solution(mesh):
    return jax.shard_map(
        shards,
        mesh=mesh,
        in_specs=(P("dp", None), P("dp", "mp"), P("dp", "mp"), P("dp", "mp"), P("dp", None)),
        out_specs=(P("dp", "mp"), P("dp", "mp"), P("dp", "mp")),
        check_vma=False,
    )
```

```python
import functools

import jax
import jax.numpy as jnp
from jax import lax
from jax.experimental import pallas as pl
from jax.experimental.pallas import tpu as pltpu
from jax.sharding import PartitionSpec as P

BLK = 128
EPSILON = 1e-06
DECAY = 0.9
STEP_SIZE = 0.005

NY, NX, NZ, NH, NC = 4, 4, 2, 4, 2
PAIRS_Y = [(0, 0), (1, 1), (2, 2), (3, 3), (0, 2), (1, 3), (0, 1), (0, 3), (1, 2), (2, 3)]
PAIRS_XZ = [(i, j) for i in range(8) for j in range(i, 8)]
F32 = jnp.float32


def move_dp(block, dy=0, dx=0, dz=0):
    route = []
    for y in range(NY):
        for x in range(NX):
            for z in range(NZ):
                target = (((y + dy) % NY) * NX + (x + dx) % NX) * NZ + (z + dz) % NZ
                route.append(((y * NX + x) * NZ + z, target))
    return lax.ppermute(block, "dp", route)


def move_mp(block, dh=0, dc=0):
    route = []
    for h in range(NH):
        for c in range(NC):
            route.append((h * NC + c, ((h + dh) % NH) * NC + (c + dc) % NC))
    return lax.ppermute(block, "mp", route)


def sum_cores(part):
    return part + move_mp(part, dc=1)


def sum_z(part):
    one, two, three = move_mp(part, dh=1), move_mp(part, dh=2), move_mp(part, dh=3)
    return (part + two) + (one + three)


def grads_kernel(
    place, tokens_ref, mine_ref, other_ref, o0_ref, o1_ref, o2_ref, o2b_ref, o3_ref, grads_ref, gram_ref, turned_ref, sums_ref
):
    step = pl.program_id(0)

    @pl.when(step == 0)
    def _():
        sums_ref[...] = jnp.zeros_like(sums_ref)
        for j in range(NH):
            for which, ref in ((0, mine_ref), (1, other_ref)):
                side = place[4] if which == 0 else 1 - place[4]
                block = lax.rem(place[3] - j + NH, NH) * 2 + side
                at = pl.ds(pl.multiple_of(block * BLK, BLK), BLK)
                for k, cols in enumerate([tokens_ref[:, at], ref[j, 0], ref[j, 1], ref[j, 2]]):
                    turned_ref[k, at, :] = cols.T

    blocks, _, _, span = grads_ref.shape
    o2 = jnp.where(step < pl.num_programs(0) // 2, o2_ref[...], o2b_ref[...])
    for k, out in enumerate((o0_ref[...], o1_ref[...], o2, o3_ref[...])):
        product = jnp.dot(turned_ref[k], out, preferred_element_type=F32)
        grads_ref[:, k] = product.reshape(blocks, BLK, span)

    def one_block(m, _):
        sums = [sums_ref[m, n] for n in range(len(PAIRS_Y))]
        for t in range(BLK // 8):
            for part in range(span // 128):
                at, lanes = pl.ds(t * 8, 8), pl.ds(part * 128, 128)
                g = [grads_ref[m, k, at, lanes] for k in range(4)]
                for n, (i, j) in enumerate(PAIRS_Y):
                    sums[n] = sums[n] + g[i] * g[j]
        for n in range(len(PAIRS_Y)):
            sums_ref[m, n] = sums[n]
        return 0

    lax.fori_loop(0, blocks, one_block, 0)

    @pl.when(step == pl.num_programs(0) - 1)
    def _():
        rows = jnp.sum(sums_ref[...], axis=2).reshape(blocks * 16, 128)
        gram_ref[...] = jnp.broadcast_to(jnp.sum(rows.T, axis=0, keepdims=True), gram_ref.shape)


def grads_and_gram(place, tokens, mine, other, outs):
    tok_dev, cols = outs[0].shape
    span = 256
    blocks = NH * NC
    half = cols // span // 2
    out_cols = pl.BlockSpec((tok_dev, span), lambda n, p: (0, n))
    first_half = pl.BlockSpec((tok_dev, span), lambda n, p: (0, jnp.minimum(n, half - 1)))
    last_half = pl.BlockSpec((tok_dev, span), lambda n, p: (0, jnp.maximum(n - half, 0)))
    landed = pl.BlockSpec(mine.shape, lambda n, p: (0, 0, 0, 0))
    return pl.pallas_call(
        grads_kernel,
        grid_spec=pltpu.PrefetchScalarGridSpec(
            num_scalar_prefetch=1,
            grid=(cols // span,),
            in_specs=[pl.BlockSpec((tok_dev, blocks * BLK), lambda n, p: (0, p[0])), landed, landed]
            + [out_cols, out_cols, first_half, last_half, out_cols],
            out_specs=[
                pl.BlockSpec((blocks, 4, BLK, span), lambda n, p: (0, 0, 0, n)),
                pl.BlockSpec((8, 128), lambda n, p: (0, 0)),
            ],
            scratch_shapes=[
                pltpu.VMEM((4, blocks * BLK, tok_dev), jnp.bfloat16),
                pltpu.VMEM((blocks, 16, 8, 128), F32),
            ],
        ),
        out_shape=[
            pltpu.VMEM((blocks, 4, BLK, cols), F32),
            jax.ShapeDtypeStruct((8, 128), F32),
        ],
        compiler_params=pltpu.CompilerParams(vmem_limit_bytes=44 * 2**20),
    )(place, tokens, mine, other, outs[0], outs[1], *outs[2], outs[3])


def mix_kernel(tok_dev, gram_ref, grads_ref, coded_ref):
    step = pl.program_id(0)
    g = gram_ref[...] * (1.0 / (tok_dev * tok_dev))
    at = {}
    for n, pair in enumerate(PAIRS_Y):
        at[pair] = g if n == 0 else pltpu.roll(g, 128 - n, 1)
    p = [at[(k, k)] for k in range(4)]
    c02, c13 = at[(0, 2)], at[(1, 3)]
    a0 = 1.0 - c02 / (2.0 * (p[0] + EPSILON))
    a2 = 1.0 - c02 / (2.0 * (p[2] + EPSILON))
    a1 = 1.0 - c13 / (2.0 * (p[1] + EPSILON))
    a3 = 1.0 - c13 / (2.0 * (p[3] + EPSILON))
    even = jnp.maximum((a0 * a0) * p[0] + 2.0 * ((a0 * a2) * c02) + (a2 * a2) * p[2], 0.0)
    odd = jnp.maximum((a1 * a1) * p[1] + 2.0 * ((a1 * a3) * c13) + (a3 * a3) * p[3], 0.0)
    cross = (a0 * a1) * at[(0, 1)] + (a0 * a3) * at[(0, 3)] + (a2 * a1) * at[(1, 2)] + (a2 * a3) * at[(2, 3)]
    f_even = 1.0 - cross / (2.0 * (even + EPSILON))
    f_odd = 1.0 - cross / (2.0 * (odd + EPSILON))
    w = [f_even * a0, f_odd * a1, f_even * a2, f_odd * a3]
    here = lax.broadcasted_iota(jnp.int32, g.shape, 1) == step * 16
    s = [
        jnp.sum(jnp.where(here, w[k] * (1.0 / tok_dev), 0.0), axis=1, keepdims=True)[:1] for k in range(4)
    ]
    span = 128
    for first in range(0, grads_ref.shape[3], span):
        lanes = pl.ds(first, span)
        mixed = (s[0] * grads_ref[0, 0, :, lanes] + s[2] * grads_ref[0, 2, :, lanes]) + (
            s[1] * grads_ref[0, 1, :, lanes] + s[3] * grads_ref[0, 3, :, lanes]
        )
        peak = jnp.maximum(jnp.max(jnp.abs(mixed), axis=0, keepdims=True), 1e-30)
        exponent = jnp.ceil(jnp.log2(peak))
        mantissa = jnp.ceil(peak * jnp.exp2(-exponent) * 512.0) * (1.0 / 512.0)
        level = mixed * (LEVELS * jnp.exp2(-exponent) / mantissa)
        size = jnp.abs(level)
        whole = jnp.floor(size)
        code = jnp.exp2(whole - 14.0) * (1.0 + (size - whole))
        coded_ref[0, :BLK, lanes] = jnp.where(level < 0.0, -code, code)
        row = lax.broadcasted_iota(jnp.int32, (8, span), 0)
        coded_ref[0, BLK:, lanes] = jnp.where(row == 0, exponent, mantissa)


LEVELS = 29.9


def decode(landed):
    code = landed[:, :BLK].astype(F32)
    exponent = landed[:, BLK : BLK + 1].astype(F32)
    mantissa = landed[:, BLK + 1 : BLK + 2].astype(F32)
    size = jnp.abs(code)
    whole = jnp.floor(jnp.log2(size))
    level = (whole + 13.0) + size * jnp.exp2(-whole)
    return jnp.where(code < 0.0, -level, level) * (jnp.exp2(exponent) * mantissa * (1.0 / LEVELS))


def mix(gram, grads, tok_dev):
    blocks, _, _, cols = grads.shape
    return pl.pallas_call(
        functools.partial(mix_kernel, tok_dev),
        grid=(blocks,),
        in_specs=[
            pl.BlockSpec((8, 128), lambda m: (0, 0)),
            pl.BlockSpec((1, 4, BLK, cols), lambda m: (m, 0, 0, 0)),
        ],
        out_specs=pl.BlockSpec((1, BLK + 8, cols), lambda m: (m, 0, 0)),
        out_shape=jax.ShapeDtypeStruct((blocks, BLK + 8, cols), F32),
        compiler_params=pltpu.CompilerParams(vmem_limit_bytes=16 * 2**20),
    )(gram, grads)


def gram8_kernel(parts_ref, gram_ref):
    def tile(t, sums):
        at = pl.ds(pl.multiple_of(t * 8, 8), 8)
        sums = list(sums)
        for span in range(parts_ref.shape[2] // 128):
            h = [parts_ref[k, at, pl.ds(span * 128, 128)] for k in range(8)]
            for n, (i, j) in enumerate(PAIRS_XZ):
                sums[n] = sums[n] + h[i] * h[j]
        return tuple(sums)

    zero = tuple(jnp.zeros((8, 128), F32) for _ in PAIRS_XZ)
    sums = lax.fori_loop(0, BLK // 8, tile, zero)
    for n, s in enumerate(sums):
        gram_ref[n : n + 1, :] = jnp.sum(s, axis=0, keepdims=True)
    gram_ref[len(sums) :, :] = jnp.zeros((gram_ref.shape[0] - len(sums), 128), F32)


def gram8(parts):
    return pl.pallas_call(
        gram8_kernel,
        out_shape=jax.ShapeDtypeStruct((40, 128), F32),
        compiler_params=pltpu.CompilerParams(vmem_limit_bytes=32 * 2**20),
    )(parts)


def update_kernel(gram_ref, parts_ref, weight_ref, momentum_ref, new_weight_ref, new_momentum_ref, half_ref):
    sums = jnp.sum(gram_ref[...], axis=1, keepdims=True)
    g = {}
    for n, (i, j) in enumerate(PAIRS_XZ):
        g[i, j] = g[j, i] = sums[n : n + 1, :]
    w = [None] * 8
    groups = [[k] for k in range(8)]
    while len(groups) > 1:
        half = len(groups) // 2
        factor = {}
        for a in range(half):
            b = a + half
            factor[a] = 1.0 - g[a, b] / (2.0 * (g[a, a] + EPSILON))
            factor[b] = 1.0 - g[a, b] / (2.0 * (g[b, b] + EPSILON))
        for a, members in enumerate(groups):
            for k in members:
                w[k] = factor[a] if w[k] is None else w[k] * factor[a]
        scaled = {(i, j): (factor[i] * factor[j]) * g[i, j] for i in factor for j in factor}
        g = {}
        for a in range(half):
            for b in range(half):
                total = (scaled[a, b] + scaled[a + half, b + half]) + (scaled[a, b + half] + scaled[a + half, b])
                g[a, b] = jnp.maximum(total, 0.0) if a == b else total
        groups = [groups[a] + groups[a + half] for a in range(half)]
    combined = w[0] * parts_ref[0]
    for k in range(1, 8):
        combined = combined + w[k] * parts_ref[k]
    new_momentum = DECAY * momentum_ref[...] + combined
    new_weight = weight_ref[...] - STEP_SIZE * new_momentum
    new_momentum_ref[...] = new_momentum
    new_weight_ref[...] = new_weight
    half_ref[...] = new_weight.astype(jnp.bfloat16)


def update(gram, parts, weight, momentum):
    rows, cols = weight.shape
    tile = 32
    flat = pl.BlockSpec((tile, cols), lambda t: (t, 0))
    return pl.pallas_call(
        update_kernel,
        grid=(rows // tile,),
        in_specs=[
            pl.BlockSpec(gram.shape, lambda t: (0, 0)),
            pl.BlockSpec((8, tile, cols), lambda t: (0, t, 0)),
            flat,
            flat,
        ],
        out_specs=[flat, flat, flat],
        out_shape=[
            jax.ShapeDtypeStruct((rows, cols), F32),
            jax.ShapeDtypeStruct((rows, cols), F32),
            jax.ShapeDtypeStruct((rows, cols), jnp.bfloat16),
        ],
        compiler_params=pltpu.CompilerParams(vmem_limit_bytes=32 * 2**20),
    )(gram, parts, weight, momentum)


def depth_block(place, j, i, e):
    y, x, z = place[0], place[1], place[2]
    return (lax.rem(y - j + NY, NY) * NX + lax.rem(x - i + NX, NX)) * NZ + lax.rem(z + e, NZ)


def project_kernel(units, start, last, place, *refs):
    mine, other = refs[:NX], refs[NX : 2 * NX]
    held, rest = refs[2 * NX : 2 * NX + units], refs[2 * NX + units :]
    total_ref = rest[-1]
    step = pl.program_id(0)

    @pl.when(step == 0)
    def _():
        total_ref[...] = rest[0][...] if start else jnp.zeros_like(total_ref)

    unit = held[0][...]
    for u in range(1, units):
        unit = jnp.where(step == u, held[u][...], unit)
    rows = total_ref.shape[1]
    for side, refs_of in enumerate((mine, other)):
        left = jnp.concatenate([ref[...] for ref in refs_of], 1)
        total_ref[side] += jnp.dot(left, unit, preferred_element_type=F32)

    if last:

        @pl.when(step == units - 1)
        def _():
            part = rows // NX
            for k in range(NX):
                first = pl.multiple_of(lax.rem(place[1] + k, NX) * part, part)
                rest[1 + k][...] = total_ref[:, pl.ds(first, part), :].astype(rest[1 + k].dtype)


def project(place, mine, other, held, start, first, stride, last):
    units = len(held)
    rows, cols = mine.shape[0], held[0].shape[1]
    shape = (2, rows, cols)
    begin = [] if start is None else [start]
    left = [
        pl.BlockSpec(
            (rows, BLK),
            lambda u, p, i=i: (0, depth_block(p, first[0] + u * stride[0], i, first[1] + u * stride[1])),
        )
        for i in range(NX)
    ]
    whole = lambda shape: pl.BlockSpec(shape, lambda u, p: (0,) * len(shape))
    part = (2, rows // NX, cols)
    return pl.pallas_call(
        functools.partial(project_kernel, units, len(begin), last),
        grid_spec=pltpu.PrefetchScalarGridSpec(
            num_scalar_prefetch=1,
            grid=(units,),
            in_specs=left + left + [whole(h.shape) for h in held] + [whole(shape)] * len(begin),
            out_specs=[whole(part)] * NX if last else whole(shape),
            scratch_shapes=[pltpu.VMEM(shape, F32)] if last else [],
        ),
        out_shape=[jax.ShapeDtypeStruct(part, jnp.bfloat16)] * NX if last else jax.ShapeDtypeStruct(shape, F32),
        compiler_params=pltpu.CompilerParams(vmem_limit_bytes=40 * 2**20),
    )(place, *([mine] * NX), *([other] * NX), *held, *begin)


def assemble_kernel(place, p0_ref, p1_ref, p2_ref, p3_ref, out_ref):
    _, part, cols = p0_ref.shape
    for k, ref in enumerate((p0_ref, p1_ref, p2_ref, p3_ref)):
        column = pl.multiple_of(lax.rem(place[1] - k + NX, NX) * cols, cols)
        for side in range(2):
            core = place[4] if side == 0 else 1 - place[4]
            row = pl.multiple_of(core * part, 16)
            out_ref[pl.ds(row, part), pl.ds(column, cols)] = ref[side]


def assemble(place, parts):
    _, part, cols = parts[0].shape
    return pl.pallas_call(
        assemble_kernel,
        in_specs=[pl.BlockSpec(memory_space=pltpu.SMEM)] + [pl.BlockSpec(memory_space=pltpu.VMEM)] * NX,
        out_specs=pl.BlockSpec(memory_space=pltpu.VMEM),
        out_shape=jax.ShapeDtypeStruct((2 * part, NX * cols), jnp.bfloat16),
        compiler_params=pltpu.CompilerParams(vmem_limit_bytes=16 * 2**20),
    )(place, *parts)


def gather_and_project(place, own, mine, other):
    cols = own.shape[1] // NX
    x = place[1]
    pieces = [lax.dynamic_slice_in_dim(own, ((x + k) % NX) * cols, cols, 1) for k in range(NX)]
    unit = jnp.concatenate([pieces[0]] + [move_dp(pieces[k], dx=k) for k in (1, 2, 3)], 0)
    partner = move_dp(unit, dz=1)
    own_ring = [move_dp(unit, dy=k) for k in (1, 2, 3)]
    total = project(place, mine, other, [unit, partner], None, (0, 0), (0, 1), False)
    own_ring, partner, total = lax.optimization_barrier((own_ring, partner, total))
    far_ring = [move_dp(partner, dy=k) for k in (1, 2, 3)]
    total = project(place, mine, other, own_ring, total, (1, 0), (1, 0), False)
    total, far_ring = lax.optimization_barrier((total, far_ring))
    parts = project(place, mine, other, far_ring, total, (1, 1), (1, 0), True)
    return assemble(place, [parts[0]] + [move_dp(parts[k], dx=k) for k in (1, 2, 3)])


def shards(tokens, out_grad, weight, momentum, next_tokens):
    dp, mp = lax.axis_index("dp"), lax.axis_index("mp")
    y, x, z = dp // (NX * NZ), dp // NZ % NX, dp % NZ
    tok_dev = tokens.shape[0]
    group = NX * NZ
    here = jnp.stack([y, x, z, mp // NC, mp % NC]).astype(jnp.int32)
    sent = []
    for k in (1, 2, 3):
        first = (((y + k) % NY) * group + mp) * BLK
        sent.append(lax.dynamic_slice_in_dim(tokens, first, BLK, 1))
    sent, next_tokens = lax.optimization_barrier((sent, next_tokens))
    sent = [move_dp(block, dy=k) for k, block in zip((1, 2, 3), sent)]
    next_half = lax.dynamic_slice_in_dim(next_tokens, (mp % NC) * (tok_dev // 2), tok_dev // 2, 0)
    sent, out_grad, next_half = lax.optimization_barrier((sent, out_grad, next_half))
    x_rings = [[(a * NX + k) * NZ + b for k in range(NX)] for a in range(NY) for b in range(NZ)]
    next_mine = lax.all_gather(next_half, "dp", axis_index_groups=x_rings, tiled=True)
    piece = jnp.stack(sent)
    half, middle = tok_dev // 2, out_grad.shape[1] // 2
    near = [move_dp(out_grad, dy=1), move_dp(out_grad, dy=3)]
    up, down = move_mp(piece, dh=1), move_mp(piece, dh=3)
    near, up, down = lax.optimization_barrier((near, up, down))
    far_out = [move_dp(near[0][:, :middle], dy=1), move_dp(near[1][:, middle:], dy=3)]
    far = [move_mp(up[:, :half], dh=1), move_mp(down[:, half:], dh=3)]
    far, far_out, near = lax.optimization_barrier((far, far_out, near))
    far = jnp.concatenate(far, 1)
    mine = jnp.stack([piece, up, far, down])
    other = move_mp(mine, dc=1)
    grads, gram = grads_and_gram(here, tokens, mine, other, [out_grad, near[0], far_out, near[1]])
    coded = mix(sum_z(sum_cores(gram)), grads, tok_dev).astype(jnp.float16)
    rings = [[ring * group + k for k in range(group)] for ring in range(NY)]
    landed = lax.all_to_all(coded, "dp", 0, 0, axis_index_groups=rings)
    parts = decode(landed)
    gram = sum_cores(gram8(parts))
    gram, next_mine = lax.optimization_barrier((gram, next_mine))
    next_other = move_mp(next_mine, dc=1)
    new_weight, new_momentum, weight_half = update(sum_z(gram), parts, weight, momentum)
    weight_half, next_other = lax.optimization_barrier((weight_half, next_other))
    projected = gather_and_project(here, weight_half, next_mine, next_other)
    return (new_weight, new_momentum, projected)


def solution(mesh):
    return jax.shard_map(
        shards,
        mesh=mesh,
        in_specs=(P("dp", None), P("dp", "mp"), P("dp", "mp"), P("dp", "mp"), P("dp", None)),
        out_specs=(P("dp", "mp"), P("dp", "mp"), P("dp", "mp")),
        check_vma=False,
    )
```

```python
import functools

import jax
import jax.numpy as jnp
from jax import lax
from jax.experimental import pallas as pl
from jax.experimental.pallas import tpu as pltpu
from jax.sharding import PartitionSpec as P

BLK = 128
EPSILON = 1e-06
DECAY = 0.9
STEP_SIZE = 0.005

NY, NX, NZ, NH, NC = 4, 4, 2, 4, 2
PAIRS_Y = [(0, 0), (1, 1), (2, 2), (3, 3), (0, 2), (1, 3), (0, 1), (0, 3), (1, 2), (2, 3)]
PAIRS_XZ = [(i, j) for i in range(8) for j in range(i, 8)]
F32 = jnp.float32


def move_dp(block, dy=0, dx=0, dz=0):
    route = []
    for y in range(NY):
        for x in range(NX):
            for z in range(NZ):
                target = (((y + dy) % NY) * NX + (x + dx) % NX) * NZ + (z + dz) % NZ
                route.append(((y * NX + x) * NZ + z, target))
    return lax.ppermute(block, "dp", route)


def move_mp(block, dh=0, dc=0):
    route = []
    for h in range(NH):
        for c in range(NC):
            route.append((h * NC + c, ((h + dh) % NH) * NC + (c + dc) % NC))
    return lax.ppermute(block, "mp", route)


def sum_cores(part):
    return part + move_mp(part, dc=1)


def sum_z(part):
    one, two, three = move_mp(part, dh=1), move_mp(part, dh=2), move_mp(part, dh=3)
    return (part + two) + (one + three)


def grads_kernel(
    place, tokens_ref, mine_ref, other_ref, o0_ref, o1_ref, o2_ref, o2b_ref, o3_ref, grads_ref, gram_ref, turned_ref, sums_ref
):
    step = pl.program_id(0)

    @pl.when(step == 0)
    def _():
        sums_ref[...] = jnp.zeros_like(sums_ref)
        for j in range(NH):
            for which, ref in ((0, mine_ref), (1, other_ref)):
                side = place[4] if which == 0 else 1 - place[4]
                block = lax.rem(place[3] - j + NH, NH) * 2 + side
                at = pl.ds(pl.multiple_of(block * BLK, BLK), BLK)
                for k, cols in enumerate([tokens_ref[:, at], ref[j, 0], ref[j, 1], ref[j, 2]]):
                    turned_ref[k, at, :] = cols.T

    blocks, _, _, span = grads_ref.shape
    o2 = jnp.where(step < pl.num_programs(0) // 2, o2_ref[...], o2b_ref[...])
    for k, out in enumerate((o0_ref[...], o1_ref[...], o2, o3_ref[...])):
        product = jnp.dot(turned_ref[k], out, preferred_element_type=F32)
        grads_ref[:, k] = product.reshape(blocks, BLK, span)

    def one_block(m, _):
        sums = [sums_ref[m, n] for n in range(len(PAIRS_Y))]
        for t in range(BLK // 8):
            for part in range(span // 128):
                at, lanes = pl.ds(t * 8, 8), pl.ds(part * 128, 128)
                g = [grads_ref[m, k, at, lanes] for k in range(4)]
                for n, (i, j) in enumerate(PAIRS_Y):
                    sums[n] = sums[n] + g[i] * g[j]
        for n in range(len(PAIRS_Y)):
            sums_ref[m, n] = sums[n]
        return 0

    lax.fori_loop(0, blocks, one_block, 0)

    @pl.when(step == pl.num_programs(0) - 1)
    def _():
        rows = jnp.sum(sums_ref[...], axis=2).reshape(blocks * 16, 128)
        gram_ref[...] = jnp.broadcast_to(jnp.sum(rows.T, axis=0, keepdims=True), gram_ref.shape)


def grads_and_gram(place, tokens, mine, other, outs):
    tok_dev, cols = outs[0].shape
    span = 256
    blocks = NH * NC
    half = cols // span // 2
    out_cols = pl.BlockSpec((tok_dev, span), lambda n, p: (0, n))
    first_half = pl.BlockSpec((tok_dev, span), lambda n, p: (0, jnp.minimum(n, half - 1)))
    last_half = pl.BlockSpec((tok_dev, span), lambda n, p: (0, jnp.maximum(n - half, 0)))
    landed = pl.BlockSpec(mine.shape, lambda n, p: (0, 0, 0, 0))
    return pl.pallas_call(
        grads_kernel,
        grid_spec=pltpu.PrefetchScalarGridSpec(
            num_scalar_prefetch=1,
            grid=(cols // span,),
            in_specs=[pl.BlockSpec((tok_dev, blocks * BLK), lambda n, p: (0, p[0])), landed, landed]
            + [out_cols, out_cols, first_half, last_half, out_cols],
            out_specs=[
                pl.BlockSpec((blocks, 4, BLK, span), lambda n, p: (0, 0, 0, n)),
                pl.BlockSpec((8, 128), lambda n, p: (0, 0)),
            ],
            scratch_shapes=[
                pltpu.VMEM((4, blocks * BLK, tok_dev), jnp.bfloat16),
                pltpu.VMEM((blocks, 16, 8, 128), F32),
            ],
        ),
        out_shape=[
            pltpu.VMEM((blocks, 4, BLK, cols), F32),
            jax.ShapeDtypeStruct((8, 128), F32),
        ],
        compiler_params=pltpu.CompilerParams(vmem_limit_bytes=44 * 2**20),
    )(place, tokens, mine, other, outs[0], outs[1], *outs[2], outs[3])


def mix_kernel(tok_dev, gram_ref, grads_ref, coded_ref):
    step = pl.program_id(0)
    g = gram_ref[...] * (1.0 / (tok_dev * tok_dev))
    at = {}
    for n, pair in enumerate(PAIRS_Y):
        at[pair] = g if n == 0 else pltpu.roll(g, 128 - n, 1)
    p = [at[(k, k)] for k in range(4)]
    c02, c13 = at[(0, 2)], at[(1, 3)]
    a0 = 1.0 - c02 / (2.0 * (p[0] + EPSILON))
    a2 = 1.0 - c02 / (2.0 * (p[2] + EPSILON))
    a1 = 1.0 - c13 / (2.0 * (p[1] + EPSILON))
    a3 = 1.0 - c13 / (2.0 * (p[3] + EPSILON))
    even = jnp.maximum((a0 * a0) * p[0] + 2.0 * ((a0 * a2) * c02) + (a2 * a2) * p[2], 0.0)
    odd = jnp.maximum((a1 * a1) * p[1] + 2.0 * ((a1 * a3) * c13) + (a3 * a3) * p[3], 0.0)
    cross = (a0 * a1) * at[(0, 1)] + (a0 * a3) * at[(0, 3)] + (a2 * a1) * at[(1, 2)] + (a2 * a3) * at[(2, 3)]
    f_even = 1.0 - cross / (2.0 * (even + EPSILON))
    f_odd = 1.0 - cross / (2.0 * (odd + EPSILON))
    w = [f_even * a0, f_odd * a1, f_even * a2, f_odd * a3]
    here = lax.broadcasted_iota(jnp.int32, g.shape, 1) == step * 16
    s = [
        jnp.sum(jnp.where(here, w[k] * (1.0 / tok_dev), 0.0), axis=1, keepdims=True)[:1] for k in range(4)
    ]
    span = 128
    for first in range(0, grads_ref.shape[3], span):
        lanes = pl.ds(first, span)
        mixed = (s[0] * grads_ref[0, 0, :, lanes] + s[2] * grads_ref[0, 2, :, lanes]) + (
            s[1] * grads_ref[0, 1, :, lanes] + s[3] * grads_ref[0, 3, :, lanes]
        )
        peak = jnp.maximum(jnp.max(jnp.abs(mixed), axis=0, keepdims=True), 1e-30)
        exponent = jnp.ceil(jnp.log2(peak))
        mantissa = jnp.ceil(peak * jnp.exp2(-exponent) * 512.0) * (1.0 / 512.0)
        level = mixed * (LEVELS * jnp.exp2(-exponent) / mantissa)
        size = jnp.abs(level)
        whole = jnp.floor(size)
        code = jnp.exp2(whole - 14.0) * (1.0 + (size - whole))
        coded_ref[0, :BLK, lanes] = jnp.where(level < 0.0, -code, code)
        row = lax.broadcasted_iota(jnp.int32, (8, span), 0)
        coded_ref[0, BLK:, lanes] = jnp.where(row == 0, exponent, mantissa)


LEVELS = 29.9


def decode(landed):
    code = landed[:, :BLK].astype(F32)
    exponent = landed[:, BLK : BLK + 1].astype(F32)
    mantissa = landed[:, BLK + 1 : BLK + 2].astype(F32)
    size = jnp.abs(code)
    whole = jnp.floor(jnp.log2(size))
    level = (whole + 13.0) + size * jnp.exp2(-whole)
    return jnp.where(code < 0.0, -level, level) * (jnp.exp2(exponent) * mantissa * (1.0 / LEVELS))


def mix(gram, grads, tok_dev):
    blocks, _, _, cols = grads.shape
    return pl.pallas_call(
        functools.partial(mix_kernel, tok_dev),
        grid=(blocks,),
        in_specs=[
            pl.BlockSpec((8, 128), lambda m: (0, 0)),
            pl.BlockSpec((1, 4, BLK, cols), lambda m: (m, 0, 0, 0)),
        ],
        out_specs=pl.BlockSpec((1, BLK + 8, cols), lambda m: (m, 0, 0)),
        out_shape=jax.ShapeDtypeStruct((blocks, BLK + 8, cols), F32),
        compiler_params=pltpu.CompilerParams(vmem_limit_bytes=16 * 2**20),
    )(gram, grads)


def gram8_kernel(parts_ref, gram_ref):
    def tile(t, sums):
        at = pl.ds(pl.multiple_of(t * 8, 8), 8)
        sums = list(sums)
        for span in range(parts_ref.shape[2] // 128):
            h = [parts_ref[k, at, pl.ds(span * 128, 128)] for k in range(8)]
            for n, (i, j) in enumerate(PAIRS_XZ):
                sums[n] = sums[n] + h[i] * h[j]
        return tuple(sums)

    zero = tuple(jnp.zeros((8, 128), F32) for _ in PAIRS_XZ)
    sums = lax.fori_loop(0, BLK // 8, tile, zero)
    for n, s in enumerate(sums):
        gram_ref[n : n + 1, :] = jnp.sum(s, axis=0, keepdims=True)
    gram_ref[len(sums) :, :] = jnp.zeros((gram_ref.shape[0] - len(sums), 128), F32)


def gram8(parts):
    return pl.pallas_call(
        gram8_kernel,
        out_shape=jax.ShapeDtypeStruct((40, 128), F32),
        compiler_params=pltpu.CompilerParams(vmem_limit_bytes=32 * 2**20),
    )(parts)


def update_kernel(gram_ref, parts_ref, weight_ref, momentum_ref, new_weight_ref, new_momentum_ref, half_ref):
    sums = jnp.sum(gram_ref[...], axis=1, keepdims=True)
    g = {}
    for n, (i, j) in enumerate(PAIRS_XZ):
        g[i, j] = g[j, i] = sums[n : n + 1, :]
    w = [None] * 8
    groups = [[k] for k in range(8)]
    while len(groups) > 1:
        half = len(groups) // 2
        factor = {}
        for a in range(half):
            b = a + half
            factor[a] = 1.0 - g[a, b] / (2.0 * (g[a, a] + EPSILON))
            factor[b] = 1.0 - g[a, b] / (2.0 * (g[b, b] + EPSILON))
        for a, members in enumerate(groups):
            for k in members:
                w[k] = factor[a] if w[k] is None else w[k] * factor[a]
        scaled = {(i, j): (factor[i] * factor[j]) * g[i, j] for i in factor for j in factor}
        g = {}
        for a in range(half):
            for b in range(half):
                total = (scaled[a, b] + scaled[a + half, b + half]) + (scaled[a, b + half] + scaled[a + half, b])
                g[a, b] = jnp.maximum(total, 0.0) if a == b else total
        groups = [groups[a] + groups[a + half] for a in range(half)]
    combined = w[0] * parts_ref[0]
    for k in range(1, 8):
        combined = combined + w[k] * parts_ref[k]
    new_momentum = DECAY * momentum_ref[...] + combined
    new_weight = weight_ref[...] - STEP_SIZE * new_momentum
    new_momentum_ref[...] = new_momentum
    new_weight_ref[...] = new_weight
    half_ref[...] = new_weight.astype(jnp.bfloat16)


def update(gram, parts, weight, momentum):
    rows, cols = weight.shape
    tile = 32
    flat = pl.BlockSpec((tile, cols), lambda t: (t, 0))
    return pl.pallas_call(
        update_kernel,
        grid=(rows // tile,),
        in_specs=[
            pl.BlockSpec(gram.shape, lambda t: (0, 0)),
            pl.BlockSpec((8, tile, cols), lambda t: (0, t, 0)),
            flat,
            flat,
        ],
        out_specs=[flat, flat, flat],
        out_shape=[
            jax.ShapeDtypeStruct((rows, cols), F32),
            jax.ShapeDtypeStruct((rows, cols), F32),
            jax.ShapeDtypeStruct((rows, cols), jnp.bfloat16),
        ],
        compiler_params=pltpu.CompilerParams(vmem_limit_bytes=32 * 2**20),
    )(gram, parts, weight, momentum)


def depth_block(place, j, i, e):
    y, x, z = place[0], place[1], place[2]
    return (lax.rem(y - j + NY, NY) * NX + lax.rem(x - i + NX, NX)) * NZ + lax.rem(z + e, NZ)


def project_kernel(units, start, last, place, *refs):
    mine, other = refs[:NX], refs[NX : 2 * NX]
    held, rest = refs[2 * NX : 2 * NX + units], refs[2 * NX + units :]
    total_ref = rest[-1]
    step = pl.program_id(0)

    @pl.when(step == 0)
    def _():
        total_ref[...] = rest[0][...] if start else jnp.zeros_like(total_ref)

    unit = held[0][...]
    for u in range(1, units):
        unit = jnp.where(step == u, held[u][...], unit)
    rows = total_ref.shape[1]
    for side, refs_of in enumerate((mine, other)):
        left = jnp.concatenate([ref[...] for ref in refs_of], 1)
        total_ref[side] += jnp.dot(left, unit, preferred_element_type=F32)

    if last:

        @pl.when(step == units - 1)
        def _():
            part = rows // NX
            for k in range(NX):
                first = pl.multiple_of(lax.rem(place[1] + k, NX) * part, part)
                rest[1 + k][...] = total_ref[:, pl.ds(first, part), :].astype(rest[1 + k].dtype)


def project(place, mine, other, held, start, first, stride, last):
    units = len(held)
    rows, cols = mine.shape[0], held[0].shape[1]
    shape = (2, rows, cols)
    begin = [] if start is None else [start]
    left = [
        pl.BlockSpec(
            (rows, BLK),
            lambda u, p, i=i: (0, depth_block(p, first[0] + u * stride[0], i, first[1] + u * stride[1])),
        )
        for i in range(NX)
    ]
    whole = lambda shape: pl.BlockSpec(shape, lambda u, p: (0,) * len(shape))
    part = (2, rows // NX, cols)
    return pl.pallas_call(
        functools.partial(project_kernel, units, len(begin), last),
        grid_spec=pltpu.PrefetchScalarGridSpec(
            num_scalar_prefetch=1,
            grid=(units,),
            in_specs=left + left + [whole(h.shape) for h in held] + [whole(shape)] * len(begin),
            out_specs=[whole(part)] * NX if last else whole(shape),
            scratch_shapes=[pltpu.VMEM(shape, F32)] if last else [],
        ),
        out_shape=[jax.ShapeDtypeStruct(part, jnp.bfloat16)] * NX if last else jax.ShapeDtypeStruct(shape, F32),
        compiler_params=pltpu.CompilerParams(vmem_limit_bytes=40 * 2**20),
    )(place, *([mine] * NX), *([other] * NX), *held, *begin)


def assemble_kernel(place, p0_ref, p1_ref, p2_ref, p3_ref, out_ref):
    _, part, cols = p0_ref.shape
    for k, ref in enumerate((p0_ref, p1_ref, p2_ref, p3_ref)):
        column = pl.multiple_of(lax.rem(place[1] - k + NX, NX) * cols, cols)
        for side in range(2):
            core = place[4] if side == 0 else 1 - place[4]
            row = pl.multiple_of(core * part, 16)
            out_ref[pl.ds(row, part), pl.ds(column, cols)] = ref[side]


def assemble(place, parts):
    _, part, cols = parts[0].shape
    return pl.pallas_call(
        assemble_kernel,
        in_specs=[pl.BlockSpec(memory_space=pltpu.SMEM)] + [pl.BlockSpec(memory_space=pltpu.VMEM)] * NX,
        out_specs=pl.BlockSpec(memory_space=pltpu.VMEM),
        out_shape=jax.ShapeDtypeStruct((2 * part, NX * cols), jnp.bfloat16),
        compiler_params=pltpu.CompilerParams(vmem_limit_bytes=16 * 2**20),
    )(place, *parts)


def gather_and_project(place, own, mine, other):
    cols = own.shape[1] // NX
    x = place[1]
    pieces = [lax.dynamic_slice_in_dim(own, ((x + k) % NX) * cols, cols, 1) for k in range(NX)]
    unit = jnp.concatenate([pieces[0]] + [move_dp(pieces[k], dx=k) for k in (1, 2, 3)], 0)
    partner = move_dp(unit, dz=1)
    own_ring = [move_dp(unit, dy=k) for k in (1, 2, 3)]
    total = project(place, mine, other, [unit, partner], None, (0, 0), (0, 1), False)
    own_ring, partner, total = lax.optimization_barrier((own_ring, partner, total))
    far_ring = [move_dp(partner, dy=k) for k in (1, 2, 3)]
    total = project(place, mine, other, own_ring, total, (1, 0), (1, 0), False)
    total, far_ring = lax.optimization_barrier((total, far_ring))
    parts = project(place, mine, other, far_ring, total, (1, 1), (1, 0), True)
    return assemble(place, [parts[0]] + [move_dp(parts[k], dx=k) for k in (1, 2, 3)])


def shards(tokens, out_grad, weight, momentum, next_tokens):
    dp, mp = lax.axis_index("dp"), lax.axis_index("mp")
    y, x, z = dp // (NX * NZ), dp // NZ % NX, dp % NZ
    tok_dev = tokens.shape[0]
    group = NX * NZ
    here = jnp.stack([y, x, z, mp // NC, mp % NC]).astype(jnp.int32)
    sent = []
    for k in (1, 2, 3):
        first = (((y + k) % NY) * group + mp) * BLK
        sent.append(lax.dynamic_slice_in_dim(tokens, first, BLK, 1))
    sent, next_tokens = lax.optimization_barrier((sent, next_tokens))
    sent = [move_dp(block, dy=k) for k, block in zip((1, 2, 3), sent)]
    next_half = lax.dynamic_slice_in_dim(next_tokens, (mp % NC) * (tok_dev // 2), tok_dev // 2, 0)
    out_grad, next_half = lax.optimization_barrier((out_grad, next_half))
    sent, next_half = lax.optimization_barrier((sent, next_half))
    x_rings = [[(a * NX + k) * NZ + b for k in range(NX)] for a in range(NY) for b in range(NZ)]
    next_mine = lax.all_gather(next_half, "dp", axis_index_groups=x_rings, tiled=True)
    piece = jnp.stack(sent)
    half, middle = tok_dev // 2, out_grad.shape[1] // 2
    near = [move_dp(out_grad, dy=1), move_dp(out_grad, dy=3)]
    up, down = move_mp(piece, dh=1), move_mp(piece, dh=3)
    near, up, down = lax.optimization_barrier((near, up, down))
    far_out = [move_dp(near[0][:, :middle], dy=1), move_dp(near[1][:, middle:], dy=3)]
    far = [move_mp(up[:, :half], dh=1), move_mp(down[:, half:], dh=3)]
    far, far_out, near = lax.optimization_barrier((far, far_out, near))
    far = jnp.concatenate(far, 1)
    mine = jnp.stack([piece, up, far, down])
    other = move_mp(mine, dc=1)
    grads, gram = grads_and_gram(here, tokens, mine, other, [out_grad, near[0], far_out, near[1]])
    coded = mix(sum_z(sum_cores(gram)), grads, tok_dev).astype(jnp.float16)
    rings = [[ring * group + k for k in range(group)] for ring in range(NY)]
    landed = lax.all_to_all(coded, "dp", 0, 0, axis_index_groups=rings)
    parts = decode(landed)
    gram = sum_cores(gram8(parts))
    gram, next_mine = lax.optimization_barrier((gram, next_mine))
    next_other = move_mp(next_mine, dc=1)
    new_weight, new_momentum, weight_half = update(sum_z(gram), parts, weight, momentum)
    weight_half, next_other = lax.optimization_barrier((weight_half, next_other))
    projected = gather_and_project(here, weight_half, next_mine, next_other)
    return (new_weight, new_momentum, projected)


def solution(mesh):
    return jax.shard_map(
        shards,
        mesh=mesh,
        in_specs=(P("dp", None), P("dp", "mp"), P("dp", "mp"), P("dp", "mp"), P("dp", None)),
        out_specs=(P("dp", "mp"), P("dp", "mp"), P("dp", "mp")),
        check_vma=False,
    )
```
